32 devices in a mesh: feat: 4 (over y, x), node: 8 (over z, core).
Axes of the slice: x: 2, y: 2, z: 4, core: 2. Of those that a mesh axis runs over, the one named last changes fastest.
Arguments:
- features: bfloat16 [8192, 1024], P('node', 'feat'), may hold values from -6 to 6
- tile_values: bfloat16 [8, 24, 128, 128], P('node'), may hold values from 0.0009994507 to 1
- tile_coords: int32 [8, 24, 2], P('node'), may hold values from 0 to 7, as said below
- tile_count: int32 [8], P('node'), may hold values from 8 to 24, as said below
- halo_index: int32 [8, 8, 4], P('node'), may hold values from 0 to 1023
- halo_weight: bfloat16 [8, 1024, 32], P('node'), may hold values from 0.0009994507 to 1
- first_self: bfloat16 [1024, 256], P('feat'), may hold values from -0.1875 to 0.1875
- first_neighbour: bfloat16 [1024, 256], P('feat'), may hold values from -3 to 3
- second_self: bfloat16 [256, 256], replicated, may hold values from -0.375 to 0.375
- second_neighbour: bfloat16 [256, 256], replicated, may hold values from -1.5 to 1.5
- upstream: bfloat16 [8192, 256], P(('node', 'feat')), may hold values from -6 to 6
- seed_flags: int32 [8192], P(('node', 'feat')), may hold values 0 or 1
Outputs:
- embedding: bfloat16 [8192, 256], P(('node', 'feat'))
- grad_first_self: float32 [1024, 256], P('feat')
- grad_first_neighbour: float32 [1024, 256], P('feat')
- grad_second_self: float32 [256, 256], replicated
- grad_second_neighbour: float32 [256, 256], replicated
The draws below stay inside these ranges and needn't reach their ends.
Inputs may be any that keep to these rules, and one draw needn't show every extreme that they name: `tile_coords`: the 24 slots of a partition name distinct pairs (destination block, source block) of its 8 blocks; only slots below tile_count are live. `tile_count`: some partition has all 24 slots live in every draw.
All inputs are finite; a program needn't handle non-finite values. No bound on the sum of `seed_flags` on one device may be relied on, other than what follows from the above.
Results may differ from the reference program's by a relative error of at most 0.015.
Values may be sent and summed in bfloat16 or wider, within the bound.
A program may use at most 64 MiB of HBM per device.

```python
import math
import jax
import jax.numpy as jnp
from jax import lax

D = 1024
H = 256
E = 256
BLOCK = 128
CAP = 4
NB = 8
PN = 1024
NODES = 8192
MAXT = 24
HALO = 32
N_FEAT = 4
N_NODE = 8


def shuffled_pairs(part_key):
    return jax.random.permutation(part_key, NB * NB)


def draw_tile_coords(key, part):
    key = jax.random.fold_in(key, 11)
    part_keys = jax.random.split(key, N_NODE)
    orders = jax.vmap(shuffled_pairs)(part_keys)[:, :MAXT]
    return jnp.stack([orders // NB, orders % NB], axis=-1).astype(jnp.int32)


def draw_tile_count(key, part):
    key = jax.random.fold_in(key, 12)
    count_key, pick_key = jax.random.split(key)
    counts = jax.random.randint(count_key, (N_NODE,), NB, MAXT + 1)
    busiest = jax.random.randint(pick_key, (), 0, N_NODE)
    return jnp.where(jnp.arange(N_NODE) == busiest, MAXT, counts).astype(jnp.int32)


def plant(drawn, stream_key, least, top_value):
    extent = drawn.shape
    index_at = [jax.random.randint(jax.random.fold_in(stream_key, axis), (), 0, extent[axis]) for axis in range(len(extent))]
    drawn = drawn.at[tuple(index_at)].set(least)
    longest = extent.index(max(extent))
    index_at[longest] = (index_at[longest] + 1) % extent[longest]
    return drawn.at[tuple(index_at)].set(top_value)


def levels(stream_key, extent, pieces, smallest, top_value):
    gain, own = 1.0, jax.random.fold_in(stream_key, 6)
    for axis_at, blocks in pieces:
        heights = jnp.exp(jax.random.uniform(jax.random.fold_in(own, axis_at), (blocks,), jnp.float32, smallest / len(pieces), top_value / len(pieces)))
        gain = gain * jnp.repeat(heights, extent[axis_at] // blocks).reshape([-1 if axis == axis_at else 1 for axis in range(len(extent))])
    return gain


def bell_draw(key, extent, scale, limit, shards=(), held_as=jnp.bfloat16):
    loudness = levels(key, extent, shards, -0.22, 0.18) if shards else 1.0
    values = jax.random.normal(key, extent, jnp.float32) * scale * loudness
    return jnp.minimum(jnp.maximum(values, -limit), limit).astype(held_as)


def setup_inputs(seed: int = 0) -> dict:
    arg_keys = jax.random.split(jax.random.key(seed), 13)
    return {
        "features": bell_draw(arg_keys[0], (NODES, D), 1.0, 6.0, ((0, 8), (1, 4))),
        "tile_values": jnp.clip(jnp.exp(math.log(1.0) - 6.9083047 * jax.random.uniform(arg_keys[1], (N_NODE, MAXT, BLOCK, BLOCK), jnp.float32) ** levels(arg_keys[1], (N_NODE, MAXT, BLOCK, BLOCK), ((0, 8),), -0.2, 0.2)), 0.0009994507, 1.0).astype(jnp.bfloat16),
        "tile_coords": draw_tile_coords(jax.random.fold_in(arg_keys[12], 71), 0),
        "tile_count": draw_tile_count(jax.random.fold_in(arg_keys[12], 71), 0),
        "halo_index": plant(jax.random.randint(arg_keys[4], (N_NODE, N_NODE, CAP), 0, PN), jax.random.fold_in(arg_keys[4], 1), 0, PN - 1).astype(jnp.int32),
        "halo_weight": jnp.clip(jnp.exp(math.log(1.0) - 6.9083047 * jax.random.uniform(arg_keys[5], (N_NODE, PN, HALO), jnp.float32) ** levels(arg_keys[5], (N_NODE, PN, HALO), ((0, 8),), -0.2, 0.2)), 0.0009994507, 1.0).astype(jnp.bfloat16),
        "first_self": bell_draw(arg_keys[6], (D, H), D ** -0.5, 0.1875, ((0, 4),)),
        "first_neighbour": bell_draw(arg_keys[7], (D, H), (max(D // 256, 1)) ** -0.5, 3.0, ((0, 4),)),
        "second_self": bell_draw(arg_keys[8], (H, E), H ** -0.5, 0.375),
        "second_neighbour": bell_draw(arg_keys[9], (H, E), (max(H // 16, 1)) ** -0.5, 1.5),
        "upstream": bell_draw(arg_keys[10], (NODES, E), 1.0, 6.0, ((0, 32),)),
        "seed_flags": plant((jax.random.randint(arg_keys[11], (NODES,), 0, 2) < 1).astype(jnp.int32), jax.random.fold_in(arg_keys[11], 1), 0, 1),
    }


HIGHEST_PRECISION = lax.Precision.HIGHEST

def silu_slope(value):
    sigm = jax.nn.sigmoid(value)
    return sigm * (1.0 + value * (1.0 - sigm))

def tile_sum(values, read_ids, write_ids, live_slots, source, targets):
    tile_side = values.shape[1]
    blocks = source.shape[0] // tile_side
    block_ids = jnp.arange(blocks).astype(jnp.int32)
    read_pick = (read_ids[:, None] == block_ids[None, :]).astype(jnp.float32)
    write_pick = ((write_ids[:, None] == targets[None, :]) & live_slots[:, None]).astype(jnp.float32)
    stacked = source.astype(jnp.float32).reshape(blocks, tile_side, source.shape[1])
    chosen = jnp.einsum('tb,bnw->tnw', read_pick, stacked, precision=HIGHEST_PRECISION)
    products = jnp.einsum('tij,tjw->tiw', values.astype(jnp.float32), chosen, precision=HIGHEST_PRECISION)
    running = jnp.einsum('tb,tiw->biw', write_pick, products, precision=HIGHEST_PRECISION)
    row_sums = jnp.einsum('tb,ti->bi', write_pick, lax.optimization_barrier(jnp.sum(values.astype(jnp.float32), axis=2)), precision=HIGHEST_PRECISION)
    return (running.reshape(-1, source.shape[1]), row_sums.reshape(-1))

def reference(features, tile_values, tile_coords, tile_count, halo_index, halo_weight, first_self, first_neighbour, second_self, second_neighbour, upstream, seed_flags):
    feat_width = D // N_FEAT
    partitions = features.reshape(N_NODE, PN, D)
    sources = jnp.arange(N_NODE).astype(jnp.int32)[:, None, None]
    fetched = partitions[sources, halo_index]
    boundary = jnp.transpose(fetched, (1, 0, 2, 3)).reshape(N_NODE, HALO, D)
    cot_scale = 1.0 / math.sqrt(NODES)
    targets = jnp.arange(NB).astype(jnp.int32)
    self_groups = first_self.astype(jnp.float32).reshape(N_FEAT, feat_width, H)
    neigh_groups = first_neighbour.astype(jnp.float32).reshape(N_FEAT, feat_width, H)

    def one_partition(inputs):
        node_rows, values, coords, live_count, halo_rows, weights, grad_rows, seed_rows = inputs
        live_slots = jnp.arange(values.shape[0]).astype(jnp.int32) < live_count
        numerator, tile_degree = tile_sum(values, coords[:, 1], coords[:, 0], live_slots, node_rows, targets)
        halo_part = jnp.dot(weights, halo_rows, preferred_element_type=jnp.float32)
        degree_one = 1.0 + tile_degree + lax.optimization_barrier(jnp.sum(weights.astype(jnp.float32), axis=1))
        aggregated = ((numerator + halo_part) / degree_one[:, None]).astype(jnp.bfloat16)
        rows_grouped = node_rows.astype(jnp.float32).reshape(PN, N_FEAT, feat_width)
        agg_grouped = aggregated.astype(jnp.float32).reshape(PN, N_FEAT, feat_width)
        partial_sums = jnp.einsum('ngk,gkh->gnh', rows_grouped, self_groups, precision=HIGHEST_PRECISION)
        partial_sums = partial_sums + jnp.einsum('ngk,gkh->gnh', agg_grouped, neigh_groups, precision=HIGHEST_PRECISION)
        partial_sums = lax.optimization_barrier(partial_sums.astype(jnp.bfloat16))
        preact = lax.optimization_barrier(jnp.sum(partial_sums.astype(jnp.float32), axis=0))
        hidden = jax.nn.silu(preact).astype(jnp.bfloat16)
        numer_two, degree_part = tile_sum(values, coords[:, 1], coords[:, 0], live_slots, hidden, targets)
        degree_two = 1.0 + degree_part
        neighbour_mean = (numer_two / degree_two[:, None]).astype(jnp.bfloat16)
        embedding = (jnp.dot(hidden, second_self, preferred_element_type=jnp.float32) + jnp.dot(neighbour_mean, second_neighbour, preferred_element_type=jnp.float32)).astype(jnp.bfloat16)
        cotangent = (grad_rows.astype(jnp.float32) * seed_rows.astype(jnp.float32)[:, None] * cot_scale).astype(jnp.bfloat16)
        grad_two_self = jnp.dot(hidden.T, cotangent, preferred_element_type=jnp.float32)
        grad_two_neigh = jnp.dot(neighbour_mean.T, cotangent, preferred_element_type=jnp.float32)
        scaled_grad = (jnp.dot(cotangent, second_neighbour.T, preferred_element_type=jnp.float32) / degree_two[:, None]).astype(jnp.bfloat16)
        spread_back, unused_sums = tile_sum(jnp.swapaxes(values, 1, 2), coords[:, 0], coords[:, 1], live_slots, scaled_grad, targets)
        grad_hidden = jnp.dot(cotangent, second_self.T, preferred_element_type=jnp.float32) + spread_back
        grad_preact = (grad_hidden * silu_slope(preact)).astype(jnp.bfloat16)
        grad_one_self = jnp.dot(node_rows.T, grad_preact, preferred_element_type=jnp.float32)
        grad_one_neigh = jnp.dot(aggregated.T, grad_preact, preferred_element_type=jnp.float32)
        return (embedding, grad_one_self, grad_one_neigh, grad_two_self, grad_two_neigh)
    results = lax.map(one_partition, (partitions, tile_values, tile_coords, tile_count, boundary, halo_weight, upstream.reshape(N_NODE, PN, E), seed_flags.reshape(N_NODE, PN)))
    embedding = results[0].reshape(NODES, E)
    return (embedding, lax.optimization_barrier(jnp.sum(results[1], axis=0)), lax.optimization_barrier(jnp.sum(results[2], axis=0)), lax.optimization_barrier(jnp.sum(results[3], axis=0)), lax.optimization_barrier(jnp.sum(results[4], axis=0)))
```

```python
import functools
import math

import jax
import jax.numpy as jnp
from jax import lax
from jax.experimental import pallas as pl
from jax.experimental.pallas import tpu as pltpu
from jax.sharding import PartitionSpec as P

HIGHEST_PRECISION = lax.Precision.HIGHEST


def silu_slope(value):
    sigm = jax.nn.sigmoid(value)
    return sigm * (1.0 + value * (1.0 - sigm))


def tile_sum(values, read_ids, write_ids, live_slots, source, targets):
    tile_side = values.shape[1]
    blocks = source.shape[0] // tile_side
    block_ids = jnp.arange(blocks, dtype=jnp.int32)
    read_pick = (read_ids[:, None] == block_ids[None, :]).astype(jnp.bfloat16)
    write_pick = ((write_ids[:, None] == targets[None, :]) & live_slots[:, None]).astype(
        jnp.float32
    )
    stacked = source.reshape(blocks, tile_side, source.shape[1])
    chosen = jnp.einsum(
        "tb,bnw->tnw", read_pick, stacked, preferred_element_type=jnp.float32
    ).astype(jnp.bfloat16)
    products = jnp.einsum("tij,tjw->tiw", values, chosen, preferred_element_type=jnp.float32)
    running = jnp.einsum("tb,tiw->biw", write_pick, products, precision=HIGHEST_PRECISION)
    row_sums = jnp.einsum(
        "tb,ti->bi",
        write_pick,
        jnp.sum(values, axis=2, dtype=jnp.float32),
        precision=HIGHEST_PRECISION,
    )
    return (running.reshape(-1, source.shape[1]), row_sums.reshape(-1))


def tile_matrix(values, coords, live_slots, row_ids, col_ids):
    source_pick = (coords[:, 1][:, None] == col_ids[None, :]).astype(jnp.bfloat16)
    target_pick = ((coords[:, 0][:, None] == row_ids[None, :]) & live_slots[:, None]).astype(
        jnp.bfloat16
    )
    paired = jnp.einsum(
        "tb,tc->tbc", target_pick, source_pick, preferred_element_type=jnp.float32
    ).astype(jnp.bfloat16)
    dense_tiles = jnp.einsum("tbc,tij->bicj", paired, values, preferred_element_type=jnp.float32)
    tile_side = values.shape[1]
    return dense_tiles.astype(jnp.bfloat16).reshape(
        row_ids.shape[0] * tile_side, col_ids.shape[0] * tile_side
    )


def on_device(
    features,
    tile_values,
    tile_coords,
    tile_count,
    halo_index,
    halo_weight,
    first_self,
    first_neighbour,
    second_self,
    second_neighbour,
    upstream,
    seed_flags,
):
    part_rows, feat_width = features.shape
    values = tile_values[0]
    coords = tile_coords[0]
    tile_side = values.shape[1]
    blocks = part_rows // tile_side
    own_rows = upstream.shape[0]
    own_blocks = own_rows // tile_side
    live_slots = jnp.arange(values.shape[0], dtype=jnp.int32) < tile_count[0]
    all_blocks = jnp.arange(blocks, dtype=jnp.int32)
    feat_group = lax.axis_index("feat")
    own_start = feat_group * own_rows
    own_ids = feat_group * own_blocks + jnp.arange(own_blocks, dtype=jnp.int32)
    contract = (((0,), (0,)), ((), ()))
    against = (((1,), (1,)), ((), ()))
    outgoing = jnp.take(features, halo_index[0], axis=0)
    incoming = lax.all_to_all(outgoing, "node", split_axis=0, concat_axis=0, tiled=True)
    boundary = incoming.reshape(-1, feat_width)
    numerator, tile_degree = tile_sum(
        values, coords[:, 1], coords[:, 0], live_slots, features, all_blocks
    )
    weights = halo_weight[0]
    halo_part = jnp.dot(weights, boundary, preferred_element_type=jnp.float32)
    degree_one = 1.0 + tile_degree + jnp.sum(weights, axis=1, dtype=jnp.float32)
    aggregated = ((numerator + halo_part) / degree_one[:, None]).astype(jnp.bfloat16)
    adjacency = tile_matrix(values, coords, live_slots, own_ids, all_blocks)
    degree_two = 1.0 + jnp.sum(adjacency, axis=1, dtype=jnp.float32)
    partial_sums = jnp.dot(features, first_self, preferred_element_type=jnp.float32) + jnp.dot(
        aggregated, first_neighbour, preferred_element_type=jnp.float32
    )
    preact_all = lax.psum(partial_sums.astype(jnp.bfloat16), "feat").astype(jnp.float32)
    hidden_all = jax.nn.silu(preact_all).astype(jnp.bfloat16)
    hidden_own = lax.dynamic_slice_in_dim(hidden_all, own_start, own_rows, 0)
    layer_sum = jnp.dot(adjacency, hidden_all, preferred_element_type=jnp.float32)
    neighbour_mean = (layer_sum / degree_two[:, None]).astype(jnp.bfloat16)
    embedding = (
        jnp.dot(hidden_own, second_self, preferred_element_type=jnp.float32)
        + jnp.dot(neighbour_mean, second_neighbour, preferred_element_type=jnp.float32)
    ).astype(jnp.bfloat16)
    cot_scale = 1.0 / math.sqrt(part_rows * lax.axis_size("node"))
    cotangent = (
        upstream.astype(jnp.float32) * seed_flags[:, None].astype(jnp.float32) * cot_scale
    ).astype(jnp.bfloat16)
    grad_two_self = lax.dot_general(
        hidden_own, cotangent, contract, preferred_element_type=jnp.float32
    )
    grad_two_neigh = lax.dot_general(
        neighbour_mean, cotangent, contract, preferred_element_type=jnp.float32
    )
    scaled_grad = (
        lax.dot_general(cotangent, second_neighbour, against, preferred_element_type=jnp.float32)
        / degree_two[:, None]
    ).astype(jnp.bfloat16)
    own_term = lax.dot_general(cotangent, second_self, against, preferred_element_type=jnp.float32)
    spread_back = lax.dot_general(
        adjacency, scaled_grad, contract, preferred_element_type=jnp.float32
    )
    own_part = lax.dynamic_slice_in_dim(spread_back, own_start, own_rows, 0) + own_term
    grad_partial = lax.dynamic_update_slice_in_dim(spread_back, own_part, own_start, 0)
    grad_all, grad_two_self, grad_two_neigh = (
        lax.psum(grad_partial.astype(jnp.bfloat16), "feat").astype(jnp.float32),
        lax.psum(grad_two_self.astype(jnp.bfloat16), "feat").astype(jnp.float32),
        lax.psum(grad_two_neigh.astype(jnp.bfloat16), "feat").astype(jnp.float32),
    )
    grad_preact = (grad_all * silu_slope(preact_all)).astype(jnp.bfloat16)
    grad_one_self = lax.dot_general(
        features, grad_preact, contract, preferred_element_type=jnp.float32
    )
    grad_one_neigh = lax.dot_general(
        aggregated, grad_preact, contract, preferred_element_type=jnp.float32
    )
    summed = lax.psum((grad_one_self, grad_one_neigh, grad_two_self, grad_two_neigh), "node")
    return (embedding, summed[0], summed[1], summed[2], summed[3])


FUSED_NODES = 8
HALO_ROWS = 16
MESH_ID = pl.DeviceIdType.MESH


def nn(a, b):
    return jnp.dot(a, b, preferred_element_type=jnp.float32)


def nt(a, b):
    return lax.dot_general(a, b, (((1,), (1,)), ((), ())), preferred_element_type=jnp.float32)


def step_kernel(
    groups, nodes,
    feats, tvals, coords, count, hidx, hweight, w1s, w1n, w2s, w2n, upstream, flags,
    emb_o, g1s_o, g1n_o, g2s_o, g2n_o,
    x_v, tiles, tiles_t, hw_v, w1s_v, w1n_v, w2s_v, w2n_v, up_v, slot_v, slot_s,
    adj, adj_t, numer, deg, agg, x_t, agg_t, cot, cot_t, scaled, grad_h,
    hsend, hrecv, psend, precv, pre, hid, mean, gpre,
    s1, r1s, comb1, r1z, g1fin, s2, r2s, comb2, r2z, g2fin,
    ld_sem, halo_ss, halo_rs, cot_ss, cot_rs, rs_ss, rs_rs, ag_ss, ag_rs,
    sib_ss, sib_rs, z_ss, z_rs, zg_ss, zg_rs, fg_ss, fg_rs, fw_ss, fw_rs,
):
    f = lax.axis_index("feat")
    n = lax.axis_index("node")
    zs = nodes // 2
    z, c = n // 2, n % 2
    rows, width = x_v.shape
    slots = tiles.shape[0] - 1
    side = tiles.shape[1]
    blocks = rows // side
    own = up_v.shape[0]
    units = w1s_v.shape[1]
    outs = w2s_v.shape[1]
    cap = hidx.shape[2]

    def local(src, dst, i):
        copy = pltpu.make_async_copy(src, dst, ld_sem.at[i])
        copy.start()
        return copy

    def remote(src, dst, ss, rs, where):
        return pltpu.make_async_remote_copy(
            src_ref=src, dst_ref=dst, send_sem=ss, recv_sem=rs,
            device_id=where, device_id_type=MESH_ID,
        )

    def feat_at(d):
        return lax.rem(f + d, groups)

    def feat_id(d):
        return {"feat": feat_at(d)}

    def z_at(d):
        return lax.rem(z + d, zs)

    def z_id(d):
        return {"node": z_at(d) * 2 + c}

    sib_id = {"node": z * 2 + (1 - c)}

    def own_rows(p):
        return pl.ds(pl.multiple_of(p * own, own), own)

    ld_up = local(upstream, up_v, 0)
    ld_x = local(feats, x_v, 1)
    ld_t = local(tvals.at[0], tiles.at[pl.ds(0, slots)], 2)
    ld_hw = local(hweight.at[0], hw_v, 3)
    ld_1s = local(w1s, w1s_v, 4)
    ld_1n = local(w1n, w1n_v, 5)
    ld_2s = local(w2s, w2s_v, 6)
    ld_2n = local(w2n, w2n_v, 7)

    barrier = pltpu.get_barrier_semaphore()
    for d in range(1, groups):
        pl.semaphore_signal(barrier, inc=1, device_id=feat_id(d), device_id_type=MESH_ID)
    for d in range(1, nodes):
        pl.semaphore_signal(
            barrier, inc=1, device_id={"node": lax.rem(n + d, nodes)}, device_id_type=MESH_ID
        )

    pairs = coords[0]
    key = pairs[:, 0:1] * blocks + pairs[:, 1:2]
    slot_id = lax.broadcasted_iota(jnp.int32, (slots, 128), 0)
    pair_id = lax.broadcasted_iota(jnp.int32, (slots, 128), 1)
    named = (key == pair_id) & (slot_id < count[0])
    slot_v[...] = jnp.broadcast_to(
        jnp.min(jnp.where(named, slot_id, slots), axis=0, keepdims=True), slot_v.shape
    )
    ld_slot = local(slot_v, slot_s, 8)
    tiles[slots] = jnp.zeros((side, side), jnp.bfloat16)
    tiles_t[slots] = jnp.zeros((side, side), jnp.bfloat16)

    scale = 1.0 / math.sqrt(rows * nodes)
    r_id = lax.broadcasted_iota(jnp.int32, (own, own), 0)
    c_id = lax.broadcasted_iota(jnp.int32, (own, own), 1)
    picked = jnp.where((r_id == c_id) & (flags[...] != 0), 1.0, 0.0).astype(jnp.bfloat16)
    ld_up.wait()
    cot[own_rows(f), :] = (nn(picked, up_v[...]) * scale).astype(jnp.bfloat16)
    row_id = lax.broadcasted_iota(jnp.int32, (HALO_ROWS, rows), 0)
    col_id = lax.broadcasted_iota(jnp.int32, (HALO_ROWS, rows), 1)
    parts = []
    for q in range(nodes):
        want = jnp.full((HALO_ROWS, rows), -1, jnp.int32)
        for k in range(cap):
            want = jnp.where(row_id == k, hidx[0, q, k], want)
        parts.append(jnp.where(want == col_id, 1.0, 0.0).astype(jnp.bfloat16))
    picks = jnp.concatenate(parts, axis=0)
    ld_x.wait()
    hsend[...] = nn(picks, x_v[...]).astype(jnp.bfloat16).reshape(hsend.shape)
    hrecv[n] = hsend[n]

    pl.semaphore_wait(barrier, groups - 1 + nodes - 1)
    halo_copies = []
    for d in range(1, nodes):
        q = lax.rem(n + d, nodes)
        copy = remote(hsend.at[q], hrecv.at[n], halo_ss.at[d], halo_rs.at[d], {"node": q})
        copy.start()
        halo_copies.append(copy)
    cot_copies = []
    for d in range(1, groups):
        mine = cot.at[own_rows(f)]
        copy = remote(mine, mine, cot_ss.at[d], cot_rs.at[d], feat_id(d))
        copy.start()
        cot_copies.append(copy)

    ld_t.wait()
    ld_slot.wait()
    for r in range(blocks):
        for s in range(blocks):
            adj[r * side:(r + 1) * side, s * side:(s + 1) * side] = tiles[
                slot_s[0, r * blocks + s]
            ]
    ones_a = jnp.ones((rows, 128), jnp.bfloat16)

    @pl.loop(0, groups)
    def _(d):
        at = own_rows(d)
        tile_rows = adj[at, :]
        numer[at, :] = nn(tile_rows, x_v[...])
        deg[at, :] = 1.0 + nn(tile_rows, ones_a)

    ld_hw.wait()
    ld_1s.wait()
    ld_1n.wait()
    for d, copy in enumerate(halo_copies):
        copy.wait_recv()
    halo = nodes * cap
    e_row = lax.broadcasted_iota(jnp.int32, (halo, nodes * HALO_ROWS), 0)
    e_col = lax.broadcasted_iota(jnp.int32, (halo, nodes * HALO_ROWS), 1)
    spread = (e_row // cap) * HALO_ROWS + e_row % cap
    unpad = jnp.where(spread == e_col, 1.0, 0.0).astype(jnp.bfloat16)
    bound = nn(unpad, hrecv[...].reshape(nodes * HALO_ROWS, width)).astype(jnp.bfloat16)
    ones_h = jnp.ones((halo, 128), jnp.bfloat16)

    def first_layer(p):
        at = own_rows(p)
        weights = hw_v[at, :]
        inverse = 1.0 / (deg[at, :] + nn(weights, ones_h))
        inverse = jnp.concatenate([inverse] * (width // 128), axis=1)
        mixed = ((numer[at, :] + nn(weights, bound)) * inverse).astype(jnp.bfloat16)
        agg[at, :] = mixed
        return nn(x_v[at, :], w1s_v[...]) + nn(mixed, w1n_v[...])

    rs_copies = []
    for d in range(1, groups):
        psend[d] = first_layer(feat_at(d)).astype(jnp.bfloat16)
        copy = remote(psend.at[d], precv.at[d], rs_ss.at[d], rs_rs.at[d], feat_id(d))
        copy.start()
        rs_copies.append(copy)
    total = first_layer(f)

    for k in range(groups):
        at = slice(k * own, (k + 1) * own)
        x_t[:, at] = x_v[at, :].T
        agg_t[:, at] = agg[at, :].T
    for copy in rs_copies:
        copy.wait_recv()
    for d in range(1, groups):
        total = total + precv[d].astype(jnp.float32)
    pre[own_rows(f), :] = total.astype(jnp.bfloat16)
    ag_copies = []
    for d in range(1, groups):
        mine = pre.at[own_rows(f)]
        copy = remote(mine, mine, ag_ss.at[d], ag_rs.at[d], feat_id(d))
        copy.start()
        ag_copies.append(copy)

    for t in range(slots):
        tiles_t[t] = tiles[t].T
    for r in range(blocks):
        for s in range(blocks):
            adj_t[s * side:(s + 1) * side, r * side:(r + 1) * side] = tiles_t[
                slot_s[0, r * blocks + s]
            ]
    ld_2s.wait()
    ld_2n.wait()
    for copy in cot_copies:
        copy.wait_recv()
    for k in range(groups):
        at = slice(k * own, (k + 1) * own)
        cot_t[:, at] = cot[at, :].T

    @pl.loop(0, groups)
    def _(d):
        at = own_rows(d)
        inverse = 1.0 / deg[at, :]
        deg[at, :] = inverse
        inverse = jnp.concatenate([inverse] * (units // 128), axis=1)
        scaled[at, :] = (nt(cot[at, :], w2n_v[...]) * inverse).astype(jnp.bfloat16)

    @pl.loop(0, groups)
    def _(d):
        at = own_rows(d)
        grad_h[at, :] = nt(cot[at, :], w2s_v[...]) + nn(adj_t[at, :], scaled[...])

    def activate(p):
        at = own_rows(p)
        value = pre[at, :].astype(jnp.float32)
        sigm = jax.nn.sigmoid(value)
        hid[at, :] = (value * sigm).astype(jnp.bfloat16)
        slope = sigm * (1.0 + value * (1.0 - sigm))
        gpre[at, :] = (grad_h[at, :] * slope).astype(jnp.bfloat16)

    activate(f)
    for d in range(groups - 1, 0, -1):
        ag_copies[d - 1].wait_recv()
        activate(feat_at(groups - d))

    piece = width // nodes
    for k, lhs in enumerate((x_t, agg_t)):
        grad = nn(lhs[...], gpre[...])
        for q in range(nodes):
            s1[q % 2, q // 2, k * piece:(k + 1) * piece, :] = grad[
                q * piece:(q + 1) * piece
            ].astype(jnp.bfloat16)
    sib1 = remote(s1.at[1 - c], r1s, sib_ss.at[0], sib_rs.at[0], sib_id)
    sib1.start()

    @pl.loop(0, groups)
    def _(d):
        at = own_rows(d)
        inverse = jnp.concatenate([deg[at, :]] * (units // 128), axis=1)
        mean[at, :] = (nn(adj[at, :], hid[...]) * inverse).astype(jnp.bfloat16)

    share = outs // groups
    bit = share // nodes
    cot_rows = cot_t[pl.ds(pl.multiple_of(f * share, share), share), :]
    both = (nn(cot_rows, hid[...]), nn(cot_rows, mean[...]))
    for q in range(nodes):
        s2[q % 2, q // 2] = jnp.concatenate(
            [grad[q * bit:(q + 1) * bit] for grad in both], axis=0
        ).astype(jnp.bfloat16)
    sib2 = remote(s2.at[1 - c], r2s, sib_ss.at[1], sib_rs.at[1], sib_id)
    sib2.start()

    z_copies = []
    for i, (sib, mine, theirs, comb, dest) in enumerate(
        ((sib1, s1, r1s, comb1, r1z), (sib2, s2, r2s, comb2, r2z))
    ):
        sib.wait_recv()
        comb[...] = (mine[c].astype(jnp.float32) + theirs[...].astype(jnp.float32)).astype(
            jnp.bfloat16
        )
        batch = []
        for d in range(1, zs):
            copy = remote(
                comb.at[z_at(d)], dest.at[d], z_ss.at[i, d], z_rs.at[i, d], z_id(d)
            )
            copy.start()
            batch.append(copy)
        z_copies.append(batch)

    at = own_rows(f)
    emb_o[...] = (nn(hid[at, :], w2s_v[...]) + nn(mean[at, :], w2n_v[...])).astype(jnp.bfloat16)

    gathers = []
    for i, (comb, dest, final) in enumerate(
        ((comb1, r1z, g1fin.at[c]), (comb2, r2z, g2fin.at[f, c]))
    ):
        total = comb[z].astype(jnp.float32)
        for d in range(1, zs):
            z_copies[i][d - 1].wait_recv()
            total = total + dest[d].astype(jnp.float32)
        if i == 0:
            g1fin[c, z] = total.astype(jnp.bfloat16)
        else:
            g2fin[f, c, z] = total.astype(jnp.bfloat16)
        batch = []
        for d in range(1, zs):
            copy = remote(
                final.at[z], final.at[z], zg_ss.at[i, d], zg_rs.at[i, d], z_id(d)
            )
            copy.start()
            batch.append(copy)
        gathers.append(batch)

    def forward(ref, i):
        copy = remote(ref, ref, fw_ss.at[i], fw_rs.at[i], sib_id)
        copy.start()
        return copy

    forwards = [forward(g1fin.at[c, z], 0)]
    for copy in gathers[1]:
        copy.wait_recv()
    feat_copies = []
    for d in range(1, groups):
        mine = g2fin.at[f, c]
        copy = remote(mine, mine, fg_ss.at[d], fg_rs.at[d], feat_id(d))
        copy.start()
        feat_copies.append(copy)
    forwards.append(forward(g2fin.at[f, c], 1))
    for d in range(1, zs):
        gathers[0][d - 1].wait_recv()
        forwards.append(forward(g1fin.at[c, z_at(zs - d)], 1 + d))
    for d in range(1, groups):
        feat_copies[d - 1].wait_recv()
        forwards.append(forward(g2fin.at[feat_at(groups - d), c], zs + d))
    for copy in forwards:
        copy.wait_recv()

    for q in range(nodes):
        at = slice(q * piece, (q + 1) * piece)
        g1s_o[at, :] = g1fin[q % 2, q // 2, :piece, :].astype(jnp.float32)
        g1n_o[at, :] = g1fin[q % 2, q // 2, piece:, :].astype(jnp.float32)
    for k, out in enumerate((g2s_o, g2n_o)):
        out[...] = jnp.concatenate(
            [
                g2fin[g, q % 2, q // 2].astype(jnp.float32)[k * bit:(k + 1) * bit]
                for g in range(groups)
                for q in range(nodes)
            ],
            axis=0,
        ).T

    for copy in halo_copies + cot_copies + rs_copies + ag_copies + [sib1, sib2]:
        copy.wait_send()
    for batch in z_copies + gathers:
        for copy in batch:
            copy.wait_send()
    for copy in feat_copies + forwards:
        copy.wait_send()


def fused_step(
    groups, nodes, features, tile_values, tile_coords, tile_count, halo_index, halo_weight,
    first_self, first_neighbour, second_self, second_neighbour, upstream, seed_flags,
):
    rows, width = features.shape
    slots, side = tile_values.shape[1], tile_values.shape[2]
    halo = halo_weight.shape[2]
    own, outs = upstream.shape
    units = first_self.shape[1]
    zs = nodes // 2
    piece = 2 * width // nodes
    bit = 2 * outs // groups // nodes
    b16, f32 = jnp.bfloat16, jnp.float32
    vmem, anywhere, smem = (
        pl.BlockSpec(memory_space=kind) for kind in (pltpu.VMEM, pl.ANY, pltpu.SMEM)
    )
    dma = pltpu.SemaphoreType.DMA
    scratch = [
        pltpu.VMEM((rows, width), b16),
        pltpu.VMEM((slots + 1, side, side), b16),
        pltpu.VMEM((slots + 1, side, side), b16),
        pltpu.VMEM((rows, halo), b16),
        pltpu.VMEM((width, units), b16),
        pltpu.VMEM((width, units), b16),
        pltpu.VMEM((units, outs), b16),
        pltpu.VMEM((units, outs), b16),
        pltpu.VMEM((own, outs), b16),
        pltpu.VMEM((8, 128), jnp.int32),
        pltpu.SMEM((8, 128), jnp.int32),
        pltpu.VMEM((rows, rows), b16),
        pltpu.VMEM((rows, rows), b16),
        pltpu.VMEM((rows, width), f32),
        pltpu.VMEM((rows, 128), f32),
        pltpu.VMEM((rows, width), b16),
        pltpu.VMEM((width, rows), b16),
        pltpu.VMEM((width, rows), b16),
        pltpu.VMEM((rows, outs), b16),
        pltpu.VMEM((outs, rows), b16),
        pltpu.VMEM((rows, units), b16),
        pltpu.VMEM((rows, units), f32),
        pltpu.VMEM((nodes, HALO_ROWS, width), b16),
        pltpu.VMEM((nodes, HALO_ROWS, width), b16),
        pltpu.VMEM((groups, own, units), b16),
        pltpu.VMEM((groups, own, units), b16),
        pltpu.VMEM((rows, units), b16),
        pltpu.VMEM((rows, units), b16),
        pltpu.VMEM((rows, units), b16),
        pltpu.VMEM((rows, units), b16),
        pltpu.VMEM((2, zs, piece, units), b16),
        pltpu.VMEM((zs, piece, units), b16),
        pltpu.VMEM((zs, piece, units), b16),
        pltpu.VMEM((zs, piece, units), b16),
        pltpu.VMEM((2, zs, piece, units), b16),
        pltpu.VMEM((2, zs, bit, units), b16),
        pltpu.VMEM((zs, bit, units), b16),
        pltpu.VMEM((zs, bit, units), b16),
        pltpu.VMEM((zs, bit, units), b16),
        pltpu.VMEM((groups, 2, zs, bit, units), b16),
        dma((9,)),
        dma((nodes,)), dma((nodes,)),
        dma((groups,)), dma((groups,)),
        dma((groups,)), dma((groups,)),
        dma((groups,)), dma((groups,)),
        dma((2,)), dma((2,)),
        dma((2, zs)), dma((2, zs)),
        dma((2, zs)), dma((2, zs)),
        dma((groups,)), dma((groups,)),
        dma((zs + groups,)), dma((zs + groups,)),
    ]
    return pl.pallas_call(
        functools.partial(step_kernel, groups, nodes),
        out_shape=(
            jax.ShapeDtypeStruct((own, outs), b16),
            jax.ShapeDtypeStruct((width, units), f32),
            jax.ShapeDtypeStruct((width, units), f32),
            jax.ShapeDtypeStruct((units, outs), f32),
            jax.ShapeDtypeStruct((units, outs), f32),
        ),
        in_specs=[
            anywhere, anywhere, vmem, smem, smem, anywhere, anywhere, anywhere, anywhere,
            anywhere, anywhere, vmem,
        ],
        out_specs=(vmem,) * 5,
        scratch_shapes=scratch,
        compiler_params=pltpu.CompilerParams(
            collective_id=0, has_side_effects=True, vmem_limit_bytes=40 * 1024 * 1024
        ),
    )(
        features, tile_values, tile_coords, tile_count, halo_index, halo_weight, first_self,
        first_neighbour, second_self, second_neighbour, upstream, seed_flags.reshape(1, own),
    )


def solution(mesh):
    groups, nodes = mesh.shape["feat"], mesh.shape["node"]
    step = functools.partial(fused_step, groups, nodes) if nodes <= FUSED_NODES else on_device
    in_specs = (
        P("node", "feat"),
        P("node", None, None, None),
        P("node", None, None),
        P("node"),
        P("node", None, None),
        P("node", None, None),
        P("feat", None),
        P("feat", None),
        P(),
        P(),
        P(("node", "feat"), None),
        P(("node", "feat")),
    )
    out_specs = (P(("node", "feat"), None), P("feat", None), P("feat", None), P(), P())
    return jax.shard_map(
        step, mesh=mesh, in_specs=in_specs, out_specs=out_specs, check_vma=False
    )
```

```python
import functools
import math

import jax
import jax.numpy as jnp
from jax import lax
from jax.experimental import pallas as pl
from jax.experimental.pallas import tpu as pltpu
from jax.sharding import PartitionSpec as P

HIGHEST_PRECISION = lax.Precision.HIGHEST


def silu_slope(value):
    sigm = jax.nn.sigmoid(value)
    return sigm * (1.0 + value * (1.0 - sigm))


def tile_sum(values, read_ids, write_ids, live_slots, source, targets):
    tile_side = values.shape[1]
    blocks = source.shape[0] // tile_side
    block_ids = jnp.arange(blocks, dtype=jnp.int32)
    read_pick = (read_ids[:, None] == block_ids[None, :]).astype(jnp.bfloat16)
    write_pick = ((write_ids[:, None] == targets[None, :]) & live_slots[:, None]).astype(
        jnp.float32
    )
    stacked = source.reshape(blocks, tile_side, source.shape[1])
    chosen = jnp.einsum(
        "tb,bnw->tnw", read_pick, stacked, preferred_element_type=jnp.float32
    ).astype(jnp.bfloat16)
    products = jnp.einsum("tij,tjw->tiw", values, chosen, preferred_element_type=jnp.float32)
    running = jnp.einsum("tb,tiw->biw", write_pick, products, precision=HIGHEST_PRECISION)
    row_sums = jnp.einsum(
        "tb,ti->bi",
        write_pick,
        jnp.sum(values, axis=2, dtype=jnp.float32),
        precision=HIGHEST_PRECISION,
    )
    return (running.reshape(-1, source.shape[1]), row_sums.reshape(-1))


def tile_matrix(values, coords, live_slots, row_ids, col_ids):
    source_pick = (coords[:, 1][:, None] == col_ids[None, :]).astype(jnp.bfloat16)
    target_pick = ((coords[:, 0][:, None] == row_ids[None, :]) & live_slots[:, None]).astype(
        jnp.bfloat16
    )
    paired = jnp.einsum(
        "tb,tc->tbc", target_pick, source_pick, preferred_element_type=jnp.float32
    ).astype(jnp.bfloat16)
    dense_tiles = jnp.einsum("tbc,tij->bicj", paired, values, preferred_element_type=jnp.float32)
    tile_side = values.shape[1]
    return dense_tiles.astype(jnp.bfloat16).reshape(
        row_ids.shape[0] * tile_side, col_ids.shape[0] * tile_side
    )


def on_device(
    features,
    tile_values,
    tile_coords,
    tile_count,
    halo_index,
    halo_weight,
    first_self,
    first_neighbour,
    second_self,
    second_neighbour,
    upstream,
    seed_flags,
):
    part_rows, feat_width = features.shape
    values = tile_values[0]
    coords = tile_coords[0]
    tile_side = values.shape[1]
    blocks = part_rows // tile_side
    own_rows = upstream.shape[0]
    own_blocks = own_rows // tile_side
    live_slots = jnp.arange(values.shape[0], dtype=jnp.int32) < tile_count[0]
    all_blocks = jnp.arange(blocks, dtype=jnp.int32)
    feat_group = lax.axis_index("feat")
    own_start = feat_group * own_rows
    own_ids = feat_group * own_blocks + jnp.arange(own_blocks, dtype=jnp.int32)
    contract = (((0,), (0,)), ((), ()))
    against = (((1,), (1,)), ((), ()))
    outgoing = jnp.take(features, halo_index[0], axis=0)
    incoming = lax.all_to_all(outgoing, "node", split_axis=0, concat_axis=0, tiled=True)
    boundary = incoming.reshape(-1, feat_width)
    numerator, tile_degree = tile_sum(
        values, coords[:, 1], coords[:, 0], live_slots, features, all_blocks
    )
    weights = halo_weight[0]
    halo_part = jnp.dot(weights, boundary, preferred_element_type=jnp.float32)
    degree_one = 1.0 + tile_degree + jnp.sum(weights, axis=1, dtype=jnp.float32)
    aggregated = ((numerator + halo_part) / degree_one[:, None]).astype(jnp.bfloat16)
    adjacency = tile_matrix(values, coords, live_slots, own_ids, all_blocks)
    degree_two = 1.0 + jnp.sum(adjacency, axis=1, dtype=jnp.float32)
    partial_sums = jnp.dot(features, first_self, preferred_element_type=jnp.float32) + jnp.dot(
        aggregated, first_neighbour, preferred_element_type=jnp.float32
    )
    preact_all = lax.psum(partial_sums.astype(jnp.bfloat16), "feat").astype(jnp.float32)
    hidden_all = jax.nn.silu(preact_all).astype(jnp.bfloat16)
    hidden_own = lax.dynamic_slice_in_dim(hidden_all, own_start, own_rows, 0)
    layer_sum = jnp.dot(adjacency, hidden_all, preferred_element_type=jnp.float32)
    neighbour_mean = (layer_sum / degree_two[:, None]).astype(jnp.bfloat16)
    embedding = (
        jnp.dot(hidden_own, second_self, preferred_element_type=jnp.float32)
        + jnp.dot(neighbour_mean, second_neighbour, preferred_element_type=jnp.float32)
    ).astype(jnp.bfloat16)
    cot_scale = 1.0 / math.sqrt(part_rows * lax.axis_size("node"))
    cotangent = (
        upstream.astype(jnp.float32) * seed_flags[:, None].astype(jnp.float32) * cot_scale
    ).astype(jnp.bfloat16)
    grad_two_self = lax.dot_general(
        hidden_own, cotangent, contract, preferred_element_type=jnp.float32
    )
    grad_two_neigh = lax.dot_general(
        neighbour_mean, cotangent, contract, preferred_element_type=jnp.float32
    )
    scaled_grad = (
        lax.dot_general(cotangent, second_neighbour, against, preferred_element_type=jnp.float32)
        / degree_two[:, None]
    ).astype(jnp.bfloat16)
    own_term = lax.dot_general(cotangent, second_self, against, preferred_element_type=jnp.float32)
    spread_back = lax.dot_general(
        adjacency, scaled_grad, contract, preferred_element_type=jnp.float32
    )
    own_part = lax.dynamic_slice_in_dim(spread_back, own_start, own_rows, 0) + own_term
    grad_partial = lax.dynamic_update_slice_in_dim(spread_back, own_part, own_start, 0)
    grad_all, grad_two_self, grad_two_neigh = (
        lax.psum(grad_partial.astype(jnp.bfloat16), "feat").astype(jnp.float32),
        lax.psum(grad_two_self.astype(jnp.bfloat16), "feat").astype(jnp.float32),
        lax.psum(grad_two_neigh.astype(jnp.bfloat16), "feat").astype(jnp.float32),
    )
    grad_preact = (grad_all * silu_slope(preact_all)).astype(jnp.bfloat16)
    grad_one_self = lax.dot_general(
        features, grad_preact, contract, preferred_element_type=jnp.float32
    )
    grad_one_neigh = lax.dot_general(
        aggregated, grad_preact, contract, preferred_element_type=jnp.float32
    )
    summed = lax.psum((grad_one_self, grad_one_neigh, grad_two_self, grad_two_neigh), "node")
    return (embedding, summed[0], summed[1], summed[2], summed[3])


FUSED_NODES = 8
HALO_ROWS = 16
MESH_ID = pl.DeviceIdType.MESH


def nn(a, b):
    return jnp.dot(a, b, preferred_element_type=jnp.float32)


def nt(a, b):
    return lax.dot_general(a, b, (((1,), (1,)), ((), ())), preferred_element_type=jnp.float32)


def step_kernel(
    groups, nodes,
    feats, tvals, coords, count, hidx, hweight, w1s, w1n, w2s, w2n, upstream, flags,
    emb_o, g1_o, g2_o,
    x_v, tiles, tiles_t, coords_v, flags_v, hidx_s, hw_t, hw_v, w1s_v, w1n_v, w2s_v, w2n_v, up_v, slot_v, slot_s,
    adj, adj_t, numer, deg, agg, x_t, agg_t, cot, cot_t, scaled, grad_h,
    hsend, hrecv, psend, precv, pre, hid, mean, gpre,
    s1, r1s, comb1, r1z, g1fin, s2, r2s, comb2, r2z, g2fin,
    ld_sem, halo_ss, halo_rs, cot_ss, cot_rs, rs_ss, rs_rs, ag_ss, ag_rs,
    sib_ss, sib_rs, z_ss, z_rs, zg_ss, zg_rs, fg_ss, fg_rs, fw_ss, fw_rs,
):
    f = lax.axis_index("feat")
    n = lax.axis_index("node")
    zs = nodes // 2
    z, c = n // 2, n % 2
    rows, width = x_v.shape
    slots = tiles.shape[0] - 1
    side = tiles.shape[1]
    blocks = rows // side
    own = up_v.shape[0]
    units = w1s_v.shape[1]
    outs = w2s_v.shape[1]
    cap = hidx.shape[1]

    def local(src, dst, i):
        copy = pltpu.make_async_copy(src, dst, ld_sem.at[i])
        copy.start()
        return copy

    def remote(src, dst, ss, rs, where):
        return pltpu.make_async_remote_copy(
            src_ref=src, dst_ref=dst, send_sem=ss, recv_sem=rs,
            device_id=where, device_id_type=MESH_ID,
        )

    def feat_at(d):
        return lax.rem(f + d, groups)

    def feat_id(d):
        return {"feat": feat_at(d)}

    def z_at(d):
        return lax.rem(z + d, zs)

    def z_id(d):
        return {"node": z_at(d) * 2 + c}

    sib_id = {"node": z * 2 + (1 - c)}

    def own_rows(p):
        return pl.ds(pl.multiple_of(p * own, own), own)

    ld_flags = local(flags, flags_v, 9)
    ld_up = local(upstream, up_v, 0)
    ld_hidx = local(hidx.at[0], hidx_s, 10)
    ld_coords = local(coords.at[0], coords_v, 11)
    ld_x = local(feats, x_v, 1)
    ld_t = local(tvals.at[0], tiles.at[pl.ds(0, slots)], 2)
    ld_hw = local(hweight.at[0], hw_t, 3)
    ld_1s = local(w1s, w1s_v, 4)
    ld_1n = local(w1n, w1n_v, 5)
    ld_2s = local(w2s, w2s_v, 6)
    ld_2n = local(w2n, w2n_v, 7)

    barrier = pltpu.get_barrier_semaphore()
    for d in range(1, groups):
        pl.semaphore_signal(barrier, inc=1, device_id=feat_id(d), device_id_type=MESH_ID)
    for d in range(1, nodes):
        pl.semaphore_signal(
            barrier, inc=1, device_id={"node": lax.rem(n + d, nodes)}, device_id_type=MESH_ID
        )

    ld_coords.wait()
    key = coords_v[0:1, :] * blocks + coords_v[1:2, :]
    t_row = lax.broadcasted_iota(jnp.int32, (slots, slots), 0)
    t_col = lax.broadcasted_iota(jnp.int32, (slots, slots), 1)
    key = jnp.sum(jnp.where(t_row == t_col, key, 0), axis=1, keepdims=True)
    slot_id = lax.broadcasted_iota(jnp.int32, (slots, 128), 0)
    pair_id = lax.broadcasted_iota(jnp.int32, (slots, 128), 1)
    named = (key == pair_id) & (slot_id < count[0])
    slot_v[...] = jnp.broadcast_to(
        jnp.min(jnp.where(named, slot_id, slots), axis=0, keepdims=True), slot_v.shape
    )
    ld_slot = local(slot_v, slot_s, 8)
    tiles[slots] = jnp.zeros((side, side), jnp.bfloat16)
    tiles_t[slots] = jnp.zeros((side, side), jnp.bfloat16)

    scale = 1.0 / math.sqrt(rows * nodes)
    r_id = lax.broadcasted_iota(jnp.int32, (own, own), 0)
    c_id = lax.broadcasted_iota(jnp.int32, (own, own), 1)
    ld_flags.wait()
    picked = jnp.where((r_id == c_id) & (flags_v[...] != 0), 1.0, 0.0).astype(jnp.bfloat16)
    ld_up.wait()
    cot[own_rows(f), :] = (nn(picked, up_v[...]) * scale).astype(jnp.bfloat16)
    row_id = lax.broadcasted_iota(jnp.int32, (HALO_ROWS, rows), 0)
    col_id = lax.broadcasted_iota(jnp.int32, (HALO_ROWS, rows), 1)
    parts = []
    ld_hidx.wait()
    for q in range(nodes):
        want = jnp.full((HALO_ROWS, rows), -1, jnp.int32)
        for k in range(cap):
            want = jnp.where(row_id == k, hidx_s[k, q], want)
        parts.append(jnp.where(want == col_id, 1.0, 0.0).astype(jnp.bfloat16))
    picks = jnp.concatenate(parts, axis=0)
    ld_x.wait()
    hsend[...] = nn(picks, x_v[...]).astype(jnp.bfloat16).reshape(hsend.shape)
    hrecv[n] = hsend[n]

    pl.semaphore_wait(barrier, groups - 1 + nodes - 1)
    halo_copies = []
    for d in range(1, nodes):
        q = lax.rem(n + d, nodes)
        copy = remote(hsend.at[q], hrecv.at[n], halo_ss.at[d], halo_rs.at[d], {"node": q})
        copy.start()
        halo_copies.append(copy)
    cot_copies = []
    for d in range(1, groups):
        mine = cot.at[own_rows(f)]
        copy = remote(mine, mine, cot_ss.at[d], cot_rs.at[d], feat_id(d))
        copy.start()
        cot_copies.append(copy)

    ld_t.wait()
    ld_slot.wait()
    for r in range(blocks):
        for s in range(blocks):
            adj[r * side:(r + 1) * side, s * side:(s + 1) * side] = tiles[
                slot_s[0, r * blocks + s]
            ]
    ones_a = jnp.ones((rows, 128), jnp.bfloat16)

    @pl.loop(0, groups)
    def _(d):
        at = own_rows(d)
        tile_rows = adj[at, :]
        numer[at, :] = nn(tile_rows, x_v[...])
        deg[at, :] = 1.0 + nn(tile_rows, ones_a)

    ld_hw.wait()
    hw_v[...] = hw_t[...].T
    ld_1s.wait()
    ld_1n.wait()
    for d, copy in enumerate(halo_copies):
        copy.wait_recv()
    halo = nodes * cap
    e_row = lax.broadcasted_iota(jnp.int32, (halo, nodes * HALO_ROWS), 0)
    e_col = lax.broadcasted_iota(jnp.int32, (halo, nodes * HALO_ROWS), 1)
    spread = (e_row // cap) * HALO_ROWS + e_row % cap
    unpad = jnp.where(spread == e_col, 1.0, 0.0).astype(jnp.bfloat16)
    bound = nn(unpad, hrecv[...].reshape(nodes * HALO_ROWS, width)).astype(jnp.bfloat16)
    ones_h = jnp.ones((halo, 128), jnp.bfloat16)

    def first_layer(p):
        at = own_rows(p)
        weights = hw_v[at, :]
        inverse = 1.0 / (deg[at, :] + nn(weights, ones_h))
        inverse = jnp.concatenate([inverse] * (width // 128), axis=1)
        mixed = ((numer[at, :] + nn(weights, bound)) * inverse).astype(jnp.bfloat16)
        agg[at, :] = mixed
        return nn(x_v[at, :], w1s_v[...]) + nn(mixed, w1n_v[...])

    rs_copies = []
    for d in range(1, groups):
        psend[d] = first_layer(feat_at(d)).astype(jnp.bfloat16)
        copy = remote(psend.at[d], precv.at[d], rs_ss.at[d], rs_rs.at[d], feat_id(d))
        copy.start()
        rs_copies.append(copy)
    total = first_layer(f)

    for k in range(groups):
        at = slice(k * own, (k + 1) * own)
        x_t[:, at] = x_v[at, :].T
        agg_t[:, at] = agg[at, :].T
    for copy in rs_copies:
        copy.wait_recv()
    for d in range(1, groups):
        total = total + precv[d].astype(jnp.float32)
    pre[own_rows(f), :] = total.astype(jnp.bfloat16)
    ag_copies = []
    for d in range(1, groups):
        mine = pre.at[own_rows(f)]
        copy = remote(mine, mine, ag_ss.at[d], ag_rs.at[d], feat_id(d))
        copy.start()
        ag_copies.append(copy)

    for t in range(slots):
        tiles_t[t] = tiles[t].T
    for r in range(blocks):
        for s in range(blocks):
            adj_t[s * side:(s + 1) * side, r * side:(r + 1) * side] = tiles_t[
                slot_s[0, r * blocks + s]
            ]
    ld_2s.wait()
    ld_2n.wait()
    for copy in cot_copies:
        copy.wait_recv()
    for k in range(groups):
        at = slice(k * own, (k + 1) * own)
        cot_t[:, at] = cot[at, :].T

    @pl.loop(0, groups)
    def _(d):
        at = own_rows(d)
        inverse = 1.0 / deg[at, :]
        deg[at, :] = inverse
        inverse = jnp.concatenate([inverse] * (units // 128), axis=1)
        scaled[at, :] = (nt(cot[at, :], w2n_v[...]) * inverse).astype(jnp.bfloat16)

    @pl.loop(0, groups)
    def _(d):
        at = own_rows(d)
        grad_h[at, :] = nt(cot[at, :], w2s_v[...]) + nn(adj_t[at, :], scaled[...])

    def activate(p):
        at = own_rows(p)
        value = pre[at, :].astype(jnp.float32)
        sigm = jax.nn.sigmoid(value)
        hid[at, :] = (value * sigm).astype(jnp.bfloat16)
        slope = sigm * (1.0 + value * (1.0 - sigm))
        gpre[at, :] = (grad_h[at, :] * slope).astype(jnp.bfloat16)

    activate(f)
    for d in range(groups - 1, 0, -1):
        ag_copies[d - 1].wait_recv()
        activate(feat_at(groups - d))

    piece = width // nodes
    for k, lhs in enumerate((x_t, agg_t)):
        grad = nn(lhs[...], gpre[...])
        for q in range(nodes):
            s1[q % 2, q // 2, k * piece:(k + 1) * piece, :] = grad[
                q * piece:(q + 1) * piece
            ].astype(jnp.bfloat16)
    sib1 = remote(s1.at[1 - c], r1s, sib_ss.at[0], sib_rs.at[0], sib_id)
    sib1.start()

    @pl.loop(0, groups)
    def _(d):
        at = own_rows(d)
        inverse = jnp.concatenate([deg[at, :]] * (units // 128), axis=1)
        mean[at, :] = (nn(adj[at, :], hid[...]) * inverse).astype(jnp.bfloat16)

    share = outs // groups
    bit = share // nodes
    cot_rows = cot_t[pl.ds(pl.multiple_of(f * share, share), share), :]
    both = (nn(cot_rows, hid[...]), nn(cot_rows, mean[...]))
    for q in range(nodes):
        s2[q % 2, q // 2] = jnp.concatenate(
            [grad[q * bit:(q + 1) * bit] for grad in both], axis=0
        ).astype(jnp.bfloat16)
    sib2 = remote(s2.at[1 - c], r2s, sib_ss.at[1], sib_rs.at[1], sib_id)
    sib2.start()

    z_copies = []
    for i, (sib, mine, theirs, comb, dest) in enumerate(
        ((sib1, s1, r1s, comb1, r1z), (sib2, s2, r2s, comb2, r2z))
    ):
        sib.wait_recv()
        comb[...] = (mine[c].astype(jnp.float32) + theirs[...].astype(jnp.float32)).astype(
            jnp.bfloat16
        )
        batch = []
        for d in range(1, zs):
            copy = remote(
                comb.at[z_at(d)], dest.at[d], z_ss.at[i, d], z_rs.at[i, d], z_id(d)
            )
            copy.start()
            batch.append(copy)
        z_copies.append(batch)

    at = own_rows(f)
    emb_o[...] = (nn(hid[at, :], w2s_v[...]) + nn(mean[at, :], w2n_v[...])).astype(jnp.bfloat16)

    gathers = []
    for i, (comb, dest, final) in enumerate(
        ((comb1, r1z, g1fin.at[c]), (comb2, r2z, g2fin.at[f, c]))
    ):
        total = comb[z].astype(jnp.float32)
        for d in range(1, zs):
            z_copies[i][d - 1].wait_recv()
            total = total + dest[d].astype(jnp.float32)
        if i == 0:
            g1fin[c, z] = total.astype(jnp.bfloat16)
        else:
            g2fin[f, c, z] = total.astype(jnp.bfloat16)
        batch = []
        for d in range(1, zs):
            copy = remote(
                final.at[z], final.at[z], zg_ss.at[i, d], zg_rs.at[i, d], z_id(d)
            )
            copy.start()
            batch.append(copy)
        gathers.append(batch)

    def forward(ref, i):
        copy = remote(ref, ref, fw_ss.at[i], fw_rs.at[i], sib_id)
        copy.start()
        return copy

    forwards = [forward(g1fin.at[c, z], 0)]
    for copy in gathers[1]:
        copy.wait_recv()
    feat_copies = []
    for d in range(1, groups):
        mine = g2fin.at[f, c]
        copy = remote(mine, mine, fg_ss.at[d], fg_rs.at[d], feat_id(d))
        copy.start()
        feat_copies.append(copy)
    forwards.append(forward(g2fin.at[f, c], 1))
    for d in range(1, zs):
        gathers[0][d - 1].wait_recv()
        forwards.append(forward(g1fin.at[c, z_at(zs - d)], 1 + d))
    for d in range(1, groups):
        feat_copies[d - 1].wait_recv()
        forwards.append(forward(g2fin.at[feat_at(groups - d), c], zs + d))
    for copy in forwards:
        copy.wait_recv()

    g1_o[...] = g1fin[...]
    g2_o[...] = g2fin[...]
    for copy in halo_copies + cot_copies + rs_copies + ag_copies + [sib1, sib2]:
        copy.wait_send()
    for batch in z_copies + gathers:
        for copy in batch:
            copy.wait_send()
    for copy in feat_copies + forwards:
        copy.wait_send()


def finish_kernel(
    groups, nodes, g1, g2, emb, emb_o, g1s_o, g1n_o, g2s_o, g2n_o, v1s, v1n, v2s, v2n, sems
):
    piece = g1.shape[2] // 2
    bit = g2.shape[3] // 2
    copies = []

    def out(src, dst):
        copy = pltpu.make_async_copy(src, dst, sems.at[len(copies)])
        copy.start()
        copies.append(copy)

    out(emb, emb_o)
    for k, (val, dst) in enumerate(((v1s, g1s_o), (v1n, g1n_o))):
        for q in range(nodes):
            val[q * piece:(q + 1) * piece, :] = g1[
                q % 2, q // 2, k * piece:(k + 1) * piece, :
            ].astype(jnp.float32)
        out(val, dst)
    for k, (val, dst) in enumerate(((v2s, g2s_o), (v2n, g2n_o))):
        val[...] = jnp.concatenate(
            [
                g2[g, q % 2, q // 2].astype(jnp.float32)[k * bit:(k + 1) * bit]
                for g in range(groups)
                for q in range(nodes)
            ],
            axis=0,
        ).T
        out(val, dst)
    for copy in copies:
        copy.wait()


def fused_step(
    groups, nodes, features, tile_values, tile_coords, tile_count, halo_index, halo_weight,
    first_self, first_neighbour, second_self, second_neighbour, upstream, seed_flags,
):
    rows, width = features.shape
    slots, side = tile_values.shape[1], tile_values.shape[2]
    halo = halo_weight.shape[2]
    own, outs = upstream.shape
    units = first_self.shape[1]
    zs = nodes // 2
    piece = 2 * width // nodes
    bit = 2 * outs // groups // nodes
    b16, f32 = jnp.bfloat16, jnp.float32
    vmem, hbm, smem = (
        pl.BlockSpec(memory_space=kind) for kind in (pltpu.VMEM, pltpu.HBM, pltpu.SMEM)
    )
    dma = pltpu.SemaphoreType.DMA
    scratch = [
        pltpu.VMEM((rows, width), b16),
        pltpu.VMEM((slots + 1, side, side), b16),
        pltpu.VMEM((slots + 1, side, side), b16),
        pltpu.VMEM((2, slots), jnp.int32),
        pltpu.VMEM((1, own), jnp.int32),
        pltpu.SMEM(halo_index.shape[:0:-1], jnp.int32),
        pltpu.VMEM((halo, rows), b16),
        pltpu.VMEM((rows, halo), b16),
        pltpu.VMEM((width, units), b16),
        pltpu.VMEM((width, units), b16),
        pltpu.VMEM((units, outs), b16),
        pltpu.VMEM((units, outs), b16),
        pltpu.VMEM((own, outs), b16),
        pltpu.VMEM((8, 128), jnp.int32),
        pltpu.SMEM((8, 128), jnp.int32),
        pltpu.VMEM((rows, rows), b16),
        pltpu.VMEM((rows, rows), b16),
        pltpu.VMEM((rows, width), f32),
        pltpu.VMEM((rows, 128), f32),
        pltpu.VMEM((rows, width), b16),
        pltpu.VMEM((width, rows), b16),
        pltpu.VMEM((width, rows), b16),
        pltpu.VMEM((rows, outs), b16),
        pltpu.VMEM((outs, rows), b16),
        pltpu.VMEM((rows, units), b16),
        pltpu.VMEM((rows, units), f32),
        pltpu.VMEM((nodes, HALO_ROWS, width), b16),
        pltpu.VMEM((nodes, HALO_ROWS, width), b16),
        pltpu.VMEM((groups, own, units), b16),
        pltpu.VMEM((groups, own, units), b16),
        pltpu.VMEM((rows, units), b16),
        pltpu.VMEM((rows, units), b16),
        pltpu.VMEM((rows, units), b16),
        pltpu.VMEM((rows, units), b16),
        pltpu.VMEM((2, zs, piece, units), b16),
        pltpu.VMEM((zs, piece, units), b16),
        pltpu.VMEM((zs, piece, units), b16),
        pltpu.VMEM((zs, piece, units), b16),
        pltpu.VMEM((2, zs, piece, units), b16),
        pltpu.VMEM((2, zs, bit, units), b16),
        pltpu.VMEM((zs, bit, units), b16),
        pltpu.VMEM((zs, bit, units), b16),
        pltpu.VMEM((zs, bit, units), b16),
        pltpu.VMEM((groups, 2, zs, bit, units), b16),
        dma((12,)),
        dma((nodes,)), dma((nodes,)),
        dma((groups,)), dma((groups,)),
        dma((groups,)), dma((groups,)),
        dma((groups,)), dma((groups,)),
        dma((2,)), dma((2,)),
        dma((2, zs)), dma((2, zs)),
        dma((2, zs)), dma((2, zs)),
        dma((groups,)), dma((groups,)),
        dma((zs + groups,)), dma((zs + groups,)),
    ]
    embedding, g1, g2 = pl.pallas_call(
        functools.partial(step_kernel, groups, nodes),
        out_shape=(
            jax.ShapeDtypeStruct((own, outs), b16),
            jax.ShapeDtypeStruct((2, zs, piece, units), b16),
            jax.ShapeDtypeStruct((groups, 2, zs, bit, units), b16),
        ),
        in_specs=[hbm, hbm, hbm, smem] + [hbm] * 8,
        out_specs=(vmem,) * 3,
        scratch_shapes=scratch,
        compiler_params=pltpu.CompilerParams(
            collective_id=0, has_side_effects=True, vmem_limit_bytes=56 * 1024 * 1024
        ),
    )(
        features, tile_values, jnp.swapaxes(tile_coords, 1, 2), tile_count,
        jnp.swapaxes(halo_index, 1, 2), jnp.swapaxes(halo_weight, 1, 2), first_self,
        first_neighbour, second_self, second_neighbour, upstream, seed_flags.reshape(1, own),
    )
    return pl.pallas_call(
        functools.partial(finish_kernel, groups, nodes),
        out_shape=(
            jax.ShapeDtypeStruct((own, outs), b16),
            jax.ShapeDtypeStruct((width, units), f32),
            jax.ShapeDtypeStruct((width, units), f32),
            jax.ShapeDtypeStruct((units, outs), f32),
            jax.ShapeDtypeStruct((units, outs), f32),
        ),
        in_specs=[vmem] * 3,
        out_specs=(hbm,) * 5,
        scratch_shapes=[
            pltpu.VMEM((width, units), f32),
            pltpu.VMEM((width, units), f32),
            pltpu.VMEM((units, outs), f32),
            pltpu.VMEM((units, outs), f32),
            dma((5,)),
        ],
    )(g1, g2, embedding)


def solution(mesh):
    groups, nodes = mesh.shape["feat"], mesh.shape["node"]
    step = functools.partial(fused_step, groups, nodes) if nodes <= FUSED_NODES else on_device
    in_specs = (
        P("node", "feat"),
        P("node", None, None, None),
        P("node", None, None),
        P("node"),
        P("node", None, None),
        P("node", None, None),
        P("feat", None),
        P("feat", None),
        P(),
        P(),
        P(("node", "feat"), None),
        P(("node", "feat")),
    )
    out_specs = (P(("node", "feat"), None), P("feat", None), P("feat", None), P(), P())
    return jax.shard_map(
        step, mesh=mesh, in_specs=in_specs, out_specs=out_specs, check_vma=False
    )
```

```python
import functools
import math

import jax
import jax.numpy as jnp
from jax import lax
from jax.experimental import pallas as pl
from jax.experimental.pallas import tpu as pltpu
from jax.sharding import PartitionSpec as P

HIGHEST_PRECISION = lax.Precision.HIGHEST


def silu_slope(value):
    sigm = jax.nn.sigmoid(value)
    return sigm * (1.0 + value * (1.0 - sigm))


def tile_sum(values, read_ids, write_ids, live_slots, source, targets):
    tile_side = values.shape[1]
    blocks = source.shape[0] // tile_side
    block_ids = jnp.arange(blocks, dtype=jnp.int32)
    read_pick = (read_ids[:, None] == block_ids[None, :]).astype(jnp.bfloat16)
    write_pick = ((write_ids[:, None] == targets[None, :]) & live_slots[:, None]).astype(
        jnp.float32
    )
    stacked = source.reshape(blocks, tile_side, source.shape[1])
    chosen = jnp.einsum(
        "tb,bnw->tnw", read_pick, stacked, preferred_element_type=jnp.float32
    ).astype(jnp.bfloat16)
    products = jnp.einsum("tij,tjw->tiw", values, chosen, preferred_element_type=jnp.float32)
    running = jnp.einsum("tb,tiw->biw", write_pick, products, precision=HIGHEST_PRECISION)
    row_sums = jnp.einsum(
        "tb,ti->bi",
        write_pick,
        jnp.sum(values, axis=2, dtype=jnp.float32),
        precision=HIGHEST_PRECISION,
    )
    return (running.reshape(-1, source.shape[1]), row_sums.reshape(-1))


def tile_matrix(values, coords, live_slots, row_ids, col_ids):
    source_pick = (coords[:, 1][:, None] == col_ids[None, :]).astype(jnp.bfloat16)
    target_pick = ((coords[:, 0][:, None] == row_ids[None, :]) & live_slots[:, None]).astype(
        jnp.bfloat16
    )
    paired = jnp.einsum(
        "tb,tc->tbc", target_pick, source_pick, preferred_element_type=jnp.float32
    ).astype(jnp.bfloat16)
    dense_tiles = jnp.einsum("tbc,tij->bicj", paired, values, preferred_element_type=jnp.float32)
    tile_side = values.shape[1]
    return dense_tiles.astype(jnp.bfloat16).reshape(
        row_ids.shape[0] * tile_side, col_ids.shape[0] * tile_side
    )


def on_device(
    features,
    tile_values,
    tile_coords,
    tile_count,
    halo_index,
    halo_weight,
    first_self,
    first_neighbour,
    second_self,
    second_neighbour,
    upstream,
    seed_flags,
):
    part_rows, feat_width = features.shape
    values = tile_values[0]
    coords = tile_coords[0]
    tile_side = values.shape[1]
    blocks = part_rows // tile_side
    own_rows = upstream.shape[0]
    own_blocks = own_rows // tile_side
    live_slots = jnp.arange(values.shape[0], dtype=jnp.int32) < tile_count[0]
    all_blocks = jnp.arange(blocks, dtype=jnp.int32)
    feat_group = lax.axis_index("feat")
    own_start = feat_group * own_rows
    own_ids = feat_group * own_blocks + jnp.arange(own_blocks, dtype=jnp.int32)
    contract = (((0,), (0,)), ((), ()))
    against = (((1,), (1,)), ((), ()))
    outgoing = jnp.take(features, halo_index[0], axis=0)
    incoming = lax.all_to_all(outgoing, "node", split_axis=0, concat_axis=0, tiled=True)
    boundary = incoming.reshape(-1, feat_width)
    numerator, tile_degree = tile_sum(
        values, coords[:, 1], coords[:, 0], live_slots, features, all_blocks
    )
    weights = halo_weight[0]
    halo_part = jnp.dot(weights, boundary, preferred_element_type=jnp.float32)
    degree_one = 1.0 + tile_degree + jnp.sum(weights, axis=1, dtype=jnp.float32)
    aggregated = ((numerator + halo_part) / degree_one[:, None]).astype(jnp.bfloat16)
    adjacency = tile_matrix(values, coords, live_slots, own_ids, all_blocks)
    degree_two = 1.0 + jnp.sum(adjacency, axis=1, dtype=jnp.float32)
    partial_sums = jnp.dot(features, first_self, preferred_element_type=jnp.float32) + jnp.dot(
        aggregated, first_neighbour, preferred_element_type=jnp.float32
    )
    preact_all = lax.psum(partial_sums.astype(jnp.bfloat16), "feat").astype(jnp.float32)
    hidden_all = jax.nn.silu(preact_all).astype(jnp.bfloat16)
    hidden_own = lax.dynamic_slice_in_dim(hidden_all, own_start, own_rows, 0)
    layer_sum = jnp.dot(adjacency, hidden_all, preferred_element_type=jnp.float32)
    neighbour_mean = (layer_sum / degree_two[:, None]).astype(jnp.bfloat16)
    embedding = (
        jnp.dot(hidden_own, second_self, preferred_element_type=jnp.float32)
        + jnp.dot(neighbour_mean, second_neighbour, preferred_element_type=jnp.float32)
    ).astype(jnp.bfloat16)
    cot_scale = 1.0 / math.sqrt(part_rows * lax.axis_size("node"))
    cotangent = (
        upstream.astype(jnp.float32) * seed_flags[:, None].astype(jnp.float32) * cot_scale
    ).astype(jnp.bfloat16)
    grad_two_self = lax.dot_general(
        hidden_own, cotangent, contract, preferred_element_type=jnp.float32
    )
    grad_two_neigh = lax.dot_general(
        neighbour_mean, cotangent, contract, preferred_element_type=jnp.float32
    )
    scaled_grad = (
        lax.dot_general(cotangent, second_neighbour, against, preferred_element_type=jnp.float32)
        / degree_two[:, None]
    ).astype(jnp.bfloat16)
    own_term = lax.dot_general(cotangent, second_self, against, preferred_element_type=jnp.float32)
    spread_back = lax.dot_general(
        adjacency, scaled_grad, contract, preferred_element_type=jnp.float32
    )
    own_part = lax.dynamic_slice_in_dim(spread_back, own_start, own_rows, 0) + own_term
    grad_partial = lax.dynamic_update_slice_in_dim(spread_back, own_part, own_start, 0)
    grad_all, grad_two_self, grad_two_neigh = (
        lax.psum(grad_partial.astype(jnp.bfloat16), "feat").astype(jnp.float32),
        lax.psum(grad_two_self.astype(jnp.bfloat16), "feat").astype(jnp.float32),
        lax.psum(grad_two_neigh.astype(jnp.bfloat16), "feat").astype(jnp.float32),
    )
    grad_preact = (grad_all * silu_slope(preact_all)).astype(jnp.bfloat16)
    grad_one_self = lax.dot_general(
        features, grad_preact, contract, preferred_element_type=jnp.float32
    )
    grad_one_neigh = lax.dot_general(
        aggregated, grad_preact, contract, preferred_element_type=jnp.float32
    )
    summed = lax.psum((grad_one_self, grad_one_neigh, grad_two_self, grad_two_neigh), "node")
    return (embedding, summed[0], summed[1], summed[2], summed[3])


FUSED_NODES = 8
HALO_ROWS = 16
MESH_ID = pl.DeviceIdType.MESH


def nn(a, b):
    return jnp.dot(a, b, preferred_element_type=jnp.float32)


def nt(a, b):
    return lax.dot_general(a, b, (((1,), (1,)), ((), ())), preferred_element_type=jnp.float32)


def step_kernel(
    groups, nodes,
    feats, tvals, coords, count, hidx, hweight, w1s, w1n, w2s, w2n, upstream, flags,
    emb_o, g1_o, g2_o,
    x_v, tiles, tiles_t, coords_v, flags_v, hidx_s, hw_t, hw_v, w1s_v, w1n_v, w2s_v, w2n_v, up_v, slot_v, slot_s,
    adj, adj_t, numer, deg, agg, x_t, agg_t, cot, cot_t, scaled, grad_h,
    hsend, hrecv, psend, precv, pre, hid, mean, gpre,
    s1, r1s, comb1, r1z, g1fin, s2, r2s, comb2, r2z, g2fin,
    ld_sem, halo_ss, halo_rs, cot_ss, cot_rs, rs_ss, rs_rs, ag_ss, ag_rs,
    sib_ss, sib_rs, z_ss, z_rs, zg_ss, zg_rs, fg_ss, fg_rs, fw_ss, fw_rs,
):
    f = lax.axis_index("feat")
    n = lax.axis_index("node")
    zs = nodes // 2
    z, c = n // 2, n % 2
    rows, width = x_v.shape
    slots = tiles.shape[0] - 1
    side = tiles.shape[1]
    blocks = rows // side
    own = up_v.shape[0]
    units = w1s_v.shape[1]
    outs = w2s_v.shape[1]
    cap = hidx.shape[1]

    def local(src, dst, i):
        copy = pltpu.make_async_copy(src, dst, ld_sem.at[i])
        copy.start()
        return copy

    def remote(src, dst, ss, rs, where):
        return pltpu.make_async_remote_copy(
            src_ref=src, dst_ref=dst, send_sem=ss, recv_sem=rs,
            device_id=where, device_id_type=MESH_ID,
        )

    def feat_at(d):
        return lax.rem(f + d, groups)

    def feat_id(d):
        return {"feat": feat_at(d)}

    def z_at(d):
        return lax.rem(z + d, zs)

    def z_id(d):
        return {"node": z_at(d) * 2 + c}

    sib_id = {"node": z * 2 + (1 - c)}

    def own_rows(p):
        return pl.ds(pl.multiple_of(p * own, own), own)

    barrier = pltpu.get_barrier_semaphore()
    for d in range(1, groups):
        pl.semaphore_signal(barrier, inc=1, device_id=feat_id(d), device_id_type=MESH_ID)
    for d in range(1, nodes):
        pl.semaphore_signal(
            barrier, inc=1, device_id={"node": lax.rem(n + d, nodes)}, device_id_type=MESH_ID
        )

    ld_flags = local(flags, flags_v, 9)
    ld_up = local(upstream, up_v, 0)
    ld_hidx = local(hidx.at[0], hidx_s, 10)
    ld_coords = local(coords.at[0], coords_v, 11)
    ld_x = local(feats, x_v, 1)
    ld_t = local(tvals.at[0], tiles.at[pl.ds(0, slots)], 2)
    ld_hw = local(hweight.at[0], hw_t, 3)
    ld_1s = local(w1s, w1s_v, 4)
    ld_1n = local(w1n, w1n_v, 5)
    ld_2s = local(w2s, w2s_v, 6)
    ld_2n = local(w2n, w2n_v, 7)

    ld_coords.wait()
    key = coords_v[0:1, :] * blocks + coords_v[1:2, :]
    t_row = lax.broadcasted_iota(jnp.int32, (slots, slots), 0)
    t_col = lax.broadcasted_iota(jnp.int32, (slots, slots), 1)
    key = jnp.sum(jnp.where(t_row == t_col, key, 0), axis=1, keepdims=True)
    slot_id = lax.broadcasted_iota(jnp.int32, (slots, 128), 0)
    pair_id = lax.broadcasted_iota(jnp.int32, (slots, 128), 1)
    named = (key == pair_id) & (slot_id < count[0])
    slot_v[...] = jnp.broadcast_to(
        jnp.min(jnp.where(named, slot_id, slots), axis=0, keepdims=True), slot_v.shape
    )
    ld_slot = local(slot_v, slot_s, 8)
    tiles[slots] = jnp.zeros((side, side), jnp.bfloat16)
    tiles_t[slots] = jnp.zeros((side, side), jnp.bfloat16)

    scale = 1.0 / math.sqrt(rows * nodes)
    r_id = lax.broadcasted_iota(jnp.int32, (own, own), 0)
    c_id = lax.broadcasted_iota(jnp.int32, (own, own), 1)
    ld_flags.wait()
    picked = jnp.where((r_id == c_id) & (flags_v[...] != 0), 1.0, 0.0).astype(jnp.bfloat16)
    ld_up.wait()
    cot[own_rows(f), :] = (nn(picked, up_v[...]) * scale).astype(jnp.bfloat16)
    pl.semaphore_wait(barrier, groups - 1 + nodes - 1)
    cot_copies = []
    for d in range(1, groups):
        mine = cot.at[own_rows(f)]
        copy = remote(mine, mine, cot_ss.at[d], cot_rs.at[d], feat_id(d))
        copy.start()
        cot_copies.append(copy)

    row_id = lax.broadcasted_iota(jnp.int32, (HALO_ROWS, rows), 0)
    col_id = lax.broadcasted_iota(jnp.int32, (HALO_ROWS, rows), 1)
    parts = []
    ld_hidx.wait()
    for q in range(nodes):
        want = jnp.full((HALO_ROWS, rows), -1, jnp.int32)
        for k in range(cap):
            want = jnp.where(row_id == k, hidx_s[k, q], want)
        parts.append(jnp.where(want == col_id, 1.0, 0.0).astype(jnp.bfloat16))
    picks = jnp.concatenate(parts, axis=0)
    ld_x.wait()
    hsend[...] = nn(picks, x_v[...]).astype(jnp.bfloat16).reshape(hsend.shape)
    hrecv[n] = hsend[n]

    halo_copies = []
    for d in range(1, nodes):
        q = lax.rem(n + d, nodes)
        copy = remote(hsend.at[q], hrecv.at[n], halo_ss.at[d], halo_rs.at[d], {"node": q})
        copy.start()
        halo_copies.append(copy)
    ld_t.wait()
    ld_slot.wait()
    for r in range(blocks):
        for s in range(blocks):
            adj[r * side:(r + 1) * side, s * side:(s + 1) * side] = tiles[
                slot_s[0, r * blocks + s]
            ]
    ones_a = jnp.ones((rows, 128), jnp.bfloat16)

    @pl.loop(0, groups)
    def _(d):
        at = own_rows(d)
        tile_rows = adj[at, :]
        numer[at, :] = nn(tile_rows, x_v[...])
        deg[at, :] = 1.0 + nn(tile_rows, ones_a)

    ld_hw.wait()
    hw_v[...] = hw_t[...].T
    ld_1s.wait()
    ld_1n.wait()
    for d, copy in enumerate(halo_copies):
        copy.wait_recv()
    halo = nodes * cap
    e_row = lax.broadcasted_iota(jnp.int32, (halo, nodes * HALO_ROWS), 0)
    e_col = lax.broadcasted_iota(jnp.int32, (halo, nodes * HALO_ROWS), 1)
    spread = (e_row // cap) * HALO_ROWS + e_row % cap
    unpad = jnp.where(spread == e_col, 1.0, 0.0).astype(jnp.bfloat16)
    bound = nn(unpad, hrecv[...].reshape(nodes * HALO_ROWS, width)).astype(jnp.bfloat16)
    ones_h = jnp.ones((halo, 128), jnp.bfloat16)

    def first_layer(p):
        at = own_rows(p)
        weights = hw_v[at, :]
        inverse = 1.0 / (deg[at, :] + nn(weights, ones_h))
        inverse = jnp.concatenate([inverse] * (width // 128), axis=1)
        mixed = ((numer[at, :] + nn(weights, bound)) * inverse).astype(jnp.bfloat16)
        agg[at, :] = mixed
        return nn(x_v[at, :], w1s_v[...]) + nn(mixed, w1n_v[...])

    rs_copies = []
    for d in range(1, groups):
        psend[d] = first_layer(feat_at(d)).astype(jnp.bfloat16)
        copy = remote(psend.at[d], precv.at[d], rs_ss.at[d], rs_rs.at[d], feat_id(d))
        copy.start()
        rs_copies.append(copy)
    total = first_layer(f)

    for copy in rs_copies:
        copy.wait_recv()
    for d in range(1, groups):
        total = total + precv[d].astype(jnp.float32)
    pre[own_rows(f), :] = total.astype(jnp.bfloat16)
    ag_copies = []
    for d in range(1, groups):
        mine = pre.at[own_rows(f)]
        copy = remote(mine, mine, ag_ss.at[d], ag_rs.at[d], feat_id(d))
        copy.start()
        ag_copies.append(copy)

    for k in range(groups):
        at = slice(k * own, (k + 1) * own)
        x_t[:, at] = x_v[at, :].T
        agg_t[:, at] = agg[at, :].T

    for t in range(slots):
        tiles_t[t] = tiles[t].T
    for r in range(blocks):
        for s in range(blocks):
            adj_t[s * side:(s + 1) * side, r * side:(r + 1) * side] = tiles_t[
                slot_s[0, r * blocks + s]
            ]
    ld_2s.wait()
    ld_2n.wait()
    for copy in cot_copies:
        copy.wait_recv()
    for k in range(groups):
        at = slice(k * own, (k + 1) * own)
        cot_t[:, at] = cot[at, :].T

    @pl.loop(0, groups)
    def _(d):
        at = own_rows(d)
        inverse = 1.0 / deg[at, :]
        deg[at, :] = inverse
        inverse = jnp.concatenate([inverse] * (units // 128), axis=1)
        scaled[at, :] = (nt(cot[at, :], w2n_v[...]) * inverse).astype(jnp.bfloat16)

    @pl.loop(0, groups)
    def _(d):
        at = own_rows(d)
        grad_h[at, :] = nt(cot[at, :], w2s_v[...]) + nn(adj_t[at, :], scaled[...])

    def activate(p):
        at = own_rows(p)
        value = pre[at, :].astype(jnp.float32)
        sigm = jax.nn.sigmoid(value)
        hid[at, :] = (value * sigm).astype(jnp.bfloat16)
        slope = sigm * (1.0 + value * (1.0 - sigm))
        gpre[at, :] = (grad_h[at, :] * slope).astype(jnp.bfloat16)

    activate(f)
    for d in range(groups - 1, 0, -1):
        ag_copies[d - 1].wait_recv()
        activate(feat_at(groups - d))

    piece = width // nodes
    for k, lhs in enumerate((x_t, agg_t)):
        grad = nn(lhs[...], gpre[...])
        for q in range(nodes):
            s1[q % 2, q // 2, k * piece:(k + 1) * piece, :] = grad[
                q * piece:(q + 1) * piece
            ].astype(jnp.bfloat16)
    sib1 = remote(s1.at[1 - c], r1s, sib_ss.at[0], sib_rs.at[0], sib_id)
    sib1.start()

    @pl.loop(0, groups)
    def _(d):
        at = own_rows(d)
        inverse = jnp.concatenate([deg[at, :]] * (units // 128), axis=1)
        mean[at, :] = (nn(adj[at, :], hid[...]) * inverse).astype(jnp.bfloat16)

    share = outs // groups
    bit = share // nodes
    cot_rows = cot_t[pl.ds(pl.multiple_of(f * share, share), share), :]
    both = (nn(cot_rows, hid[...]), nn(cot_rows, mean[...]))
    for q in range(nodes):
        s2[q % 2, q // 2] = jnp.concatenate(
            [grad[q * bit:(q + 1) * bit] for grad in both], axis=0
        ).astype(jnp.bfloat16)
    sib2 = remote(s2.at[1 - c], r2s, sib_ss.at[1], sib_rs.at[1], sib_id)
    sib2.start()

    z_copies = [None, None]
    for i, sib, mine, theirs, comb, dest in (
        (1, sib2, s2, r2s, comb2, r2z),
        (0, sib1, s1, r1s, comb1, r1z),
    ):
        sib.wait_recv()
        comb[...] = (mine[c].astype(jnp.float32) + theirs[...].astype(jnp.float32)).astype(
            jnp.bfloat16
        )
        batch = []
        for d in range(1, zs):
            copy = remote(
                comb.at[z_at(d)], dest.at[d], z_ss.at[i, d], z_rs.at[i, d], z_id(d)
            )
            copy.start()
            batch.append(copy)
        z_copies[i] = batch

    at = own_rows(f)
    emb_o[...] = (nn(hid[at, :], w2s_v[...]) + nn(mean[at, :], w2n_v[...])).astype(jnp.bfloat16)

    gathers = [None, None]
    for i, comb, dest, final in (
        (1, comb2, r2z, g2fin.at[f, c]),
        (0, comb1, r1z, g1fin.at[c]),
    ):
        total = comb[z].astype(jnp.float32)
        for d in range(1, zs):
            z_copies[i][d - 1].wait_recv()
            total = total + dest[d].astype(jnp.float32)
        if i == 0:
            g1fin[c, z] = total.astype(jnp.bfloat16)
        else:
            g2fin[f, c, z] = total.astype(jnp.bfloat16)
        batch = []
        for d in range(1, zs):
            copy = remote(
                final.at[z], final.at[z], zg_ss.at[i, d], zg_rs.at[i, d], z_id(d)
            )
            copy.start()
            batch.append(copy)
        gathers[i] = batch

    def forward(ref, i):
        copy = remote(ref, ref, fw_ss.at[i], fw_rs.at[i], sib_id)
        copy.start()
        return copy

    forwards = [forward(g1fin.at[c, z], 0)]
    for copy in gathers[1]:
        copy.wait_recv()
    feat_copies = []
    for d in range(1, groups):
        mine = g2fin.at[f, c]
        copy = remote(mine, mine, fg_ss.at[d], fg_rs.at[d], feat_id(d))
        copy.start()
        feat_copies.append(copy)
    forwards.append(forward(g2fin.at[f, c], 1))
    for d in range(1, zs):
        gathers[0][d - 1].wait_recv()
        forwards.append(forward(g1fin.at[c, z_at(zs - d)], 1 + d))
    for d in range(1, groups):
        feat_copies[d - 1].wait_recv()
        forwards.append(forward(g2fin.at[feat_at(groups - d), c], zs + d))
    for copy in forwards:
        copy.wait_recv()

    g1_o[...] = g1fin[...]
    g2_o[...] = g2fin[...]
    for copy in halo_copies + cot_copies + rs_copies + ag_copies + [sib1, sib2]:
        copy.wait_send()
    for batch in z_copies + gathers:
        for copy in batch:
            copy.wait_send()
    for copy in feat_copies + forwards:
        copy.wait_send()


def finish_kernel(
    groups, nodes, g1, g2, emb, emb_o, g1s_o, g1n_o, g2s_o, g2n_o, v1s, v1n, v2s, v2n, sems
):
    piece = g1.shape[2] // 2
    bit = g2.shape[3] // 2
    copies = []

    def out(src, dst):
        copy = pltpu.make_async_copy(src, dst, sems.at[len(copies)])
        copy.start()
        copies.append(copy)

    out(emb, emb_o)
    for k, (val, dst) in enumerate(((v1s, g1s_o), (v1n, g1n_o))):
        for q in range(nodes):
            val[q * piece:(q + 1) * piece, :] = g1[
                q % 2, q // 2, k * piece:(k + 1) * piece, :
            ].astype(jnp.float32)
        out(val, dst)
    for k, (val, dst) in enumerate(((v2s, g2s_o), (v2n, g2n_o))):
        val[...] = jnp.concatenate(
            [
                g2[g, q % 2, q // 2].astype(jnp.float32)[k * bit:(k + 1) * bit]
                for g in range(groups)
                for q in range(nodes)
            ],
            axis=0,
        ).T
        out(val, dst)
    for copy in copies:
        copy.wait()


def fused_step(
    groups, nodes, features, tile_values, tile_coords, tile_count, halo_index, halo_weight,
    first_self, first_neighbour, second_self, second_neighbour, upstream, seed_flags,
):
    rows, width = features.shape
    slots, side = tile_values.shape[1], tile_values.shape[2]
    halo = halo_weight.shape[2]
    own, outs = upstream.shape
    units = first_self.shape[1]
    zs = nodes // 2
    piece = 2 * width // nodes
    bit = 2 * outs // groups // nodes
    b16, f32 = jnp.bfloat16, jnp.float32
    vmem, hbm, smem = (
        pl.BlockSpec(memory_space=kind) for kind in (pltpu.VMEM, pltpu.HBM, pltpu.SMEM)
    )
    dma = pltpu.SemaphoreType.DMA
    scratch = [
        pltpu.VMEM((rows, width), b16),
        pltpu.VMEM((slots + 1, side, side), b16),
        pltpu.VMEM((slots + 1, side, side), b16),
        pltpu.VMEM((2, slots), jnp.int32),
        pltpu.VMEM((1, own), jnp.int32),
        pltpu.SMEM(halo_index.shape[:0:-1], jnp.int32),
        pltpu.VMEM((halo, rows), b16),
        pltpu.VMEM((rows, halo), b16),
        pltpu.VMEM((width, units), b16),
        pltpu.VMEM((width, units), b16),
        pltpu.VMEM((units, outs), b16),
        pltpu.VMEM((units, outs), b16),
        pltpu.VMEM((own, outs), b16),
        pltpu.VMEM((8, 128), jnp.int32),
        pltpu.SMEM((8, 128), jnp.int32),
        pltpu.VMEM((rows, rows), b16),
        pltpu.VMEM((rows, rows), b16),
        pltpu.VMEM((rows, width), f32),
        pltpu.VMEM((rows, 128), f32),
        pltpu.VMEM((rows, width), b16),
        pltpu.VMEM((width, rows), b16),
        pltpu.VMEM((width, rows), b16),
        pltpu.VMEM((rows, outs), b16),
        pltpu.VMEM((outs, rows), b16),
        pltpu.VMEM((rows, units), b16),
        pltpu.VMEM((rows, units), f32),
        pltpu.VMEM((nodes, HALO_ROWS, width), b16),
        pltpu.VMEM((nodes, HALO_ROWS, width), b16),
        pltpu.VMEM((groups, own, units), b16),
        pltpu.VMEM((groups, own, units), b16),
        pltpu.VMEM((rows, units), b16),
        pltpu.VMEM((rows, units), b16),
        pltpu.VMEM((rows, units), b16),
        pltpu.VMEM((rows, units), b16),
        pltpu.VMEM((2, zs, piece, units), b16),
        pltpu.VMEM((zs, piece, units), b16),
        pltpu.VMEM((zs, piece, units), b16),
        pltpu.VMEM((zs, piece, units), b16),
        pltpu.VMEM((2, zs, piece, units), b16),
        pltpu.VMEM((2, zs, bit, units), b16),
        pltpu.VMEM((zs, bit, units), b16),
        pltpu.VMEM((zs, bit, units), b16),
        pltpu.VMEM((zs, bit, units), b16),
        pltpu.VMEM((groups, 2, zs, bit, units), b16),
        dma((12,)),
        dma((nodes,)), dma((nodes,)),
        dma((groups,)), dma((groups,)),
        dma((groups,)), dma((groups,)),
        dma((groups,)), dma((groups,)),
        dma((2,)), dma((2,)),
        dma((2, zs)), dma((2, zs)),
        dma((2, zs)), dma((2, zs)),
        dma((groups,)), dma((groups,)),
        dma((zs + groups,)), dma((zs + groups,)),
    ]
    embedding, g1, g2 = pl.pallas_call(
        functools.partial(step_kernel, groups, nodes),
        out_shape=(
            jax.ShapeDtypeStruct((own, outs), b16),
            jax.ShapeDtypeStruct((2, zs, piece, units), b16),
            jax.ShapeDtypeStruct((groups, 2, zs, bit, units), b16),
        ),
        in_specs=[hbm, hbm, hbm, smem] + [hbm] * 8,
        out_specs=(vmem,) * 3,
        scratch_shapes=scratch,
        compiler_params=pltpu.CompilerParams(
            collective_id=0, has_side_effects=True, vmem_limit_bytes=56 * 1024 * 1024
        ),
    )(
        features, tile_values, jnp.swapaxes(tile_coords, 1, 2), tile_count,
        jnp.swapaxes(halo_index, 1, 2), jnp.swapaxes(halo_weight, 1, 2), first_self,
        first_neighbour, second_self, second_neighbour, upstream, seed_flags.reshape(1, own),
    )
    return pl.pallas_call(
        functools.partial(finish_kernel, groups, nodes),
        out_shape=(
            jax.ShapeDtypeStruct((own, outs), b16),
            jax.ShapeDtypeStruct((width, units), f32),
            jax.ShapeDtypeStruct((width, units), f32),
            jax.ShapeDtypeStruct((units, outs), f32),
            jax.ShapeDtypeStruct((units, outs), f32),
        ),
        in_specs=[vmem] * 3,
        out_specs=(hbm,) * 5,
        scratch_shapes=[
            pltpu.VMEM((width, units), f32),
            pltpu.VMEM((width, units), f32),
            pltpu.VMEM((units, outs), f32),
            pltpu.VMEM((units, outs), f32),
            dma((5,)),
        ],
    )(g1, g2, embedding)


def solution(mesh):
    groups, nodes = mesh.shape["feat"], mesh.shape["node"]
    step = functools.partial(fused_step, groups, nodes) if nodes <= FUSED_NODES else on_device
    in_specs = (
        P("node", "feat"),
        P("node", None, None, None),
        P("node", None, None),
        P("node"),
        P("node", None, None),
        P("node", None, None),
        P("feat", None),
        P("feat", None),
        P(),
        P(),
        P(("node", "feat"), None),
        P(("node", "feat")),
    )
    out_specs = (P(("node", "feat"), None), P("feat", None), P("feat", None), P(), P())
    return jax.shard_map(
        step, mesh=mesh, in_specs=in_specs, out_specs=out_specs, check_vma=False
    )
```

```python
import functools
import math

import jax
import jax.numpy as jnp
from jax import lax
from jax.experimental import pallas as pl
from jax.experimental.pallas import tpu as pltpu
from jax.sharding import PartitionSpec as P

HIGHEST_PRECISION = lax.Precision.HIGHEST


def silu_slope(value):
    sigm = jax.nn.sigmoid(value)
    return sigm * (1.0 + value * (1.0 - sigm))


def tile_sum(values, read_ids, write_ids, live_slots, source, targets):
    tile_side = values.shape[1]
    blocks = source.shape[0] // tile_side
    block_ids = jnp.arange(blocks, dtype=jnp.int32)
    read_pick = (read_ids[:, None] == block_ids[None, :]).astype(jnp.bfloat16)
    write_pick = ((write_ids[:, None] == targets[None, :]) & live_slots[:, None]).astype(
        jnp.float32
    )
    stacked = source.reshape(blocks, tile_side, source.shape[1])
    chosen = jnp.einsum(
        "tb,bnw->tnw", read_pick, stacked, preferred_element_type=jnp.float32
    ).astype(jnp.bfloat16)
    products = jnp.einsum("tij,tjw->tiw", values, chosen, preferred_element_type=jnp.float32)
    running = jnp.einsum("tb,tiw->biw", write_pick, products, precision=HIGHEST_PRECISION)
    row_sums = jnp.einsum(
        "tb,ti->bi",
        write_pick,
        jnp.sum(values, axis=2, dtype=jnp.float32),
        precision=HIGHEST_PRECISION,
    )
    return (running.reshape(-1, source.shape[1]), row_sums.reshape(-1))


def tile_matrix(values, coords, live_slots, row_ids, col_ids):
    source_pick = (coords[:, 1][:, None] == col_ids[None, :]).astype(jnp.bfloat16)
    target_pick = ((coords[:, 0][:, None] == row_ids[None, :]) & live_slots[:, None]).astype(
        jnp.bfloat16
    )
    paired = jnp.einsum(
        "tb,tc->tbc", target_pick, source_pick, preferred_element_type=jnp.float32
    ).astype(jnp.bfloat16)
    dense_tiles = jnp.einsum("tbc,tij->bicj", paired, values, preferred_element_type=jnp.float32)
    tile_side = values.shape[1]
    return dense_tiles.astype(jnp.bfloat16).reshape(
        row_ids.shape[0] * tile_side, col_ids.shape[0] * tile_side
    )


def on_device(
    features,
    tile_values,
    tile_coords,
    tile_count,
    halo_index,
    halo_weight,
    first_self,
    first_neighbour,
    second_self,
    second_neighbour,
    upstream,
    seed_flags,
):
    part_rows, feat_width = features.shape
    values = tile_values[0]
    coords = tile_coords[0]
    tile_side = values.shape[1]
    blocks = part_rows // tile_side
    own_rows = upstream.shape[0]
    own_blocks = own_rows // tile_side
    live_slots = jnp.arange(values.shape[0], dtype=jnp.int32) < tile_count[0]
    all_blocks = jnp.arange(blocks, dtype=jnp.int32)
    feat_group = lax.axis_index("feat")
    own_start = feat_group * own_rows
    own_ids = feat_group * own_blocks + jnp.arange(own_blocks, dtype=jnp.int32)
    contract = (((0,), (0,)), ((), ()))
    against = (((1,), (1,)), ((), ()))
    outgoing = jnp.take(features, halo_index[0], axis=0)
    incoming = lax.all_to_all(outgoing, "node", split_axis=0, concat_axis=0, tiled=True)
    boundary = incoming.reshape(-1, feat_width)
    numerator, tile_degree = tile_sum(
        values, coords[:, 1], coords[:, 0], live_slots, features, all_blocks
    )
    weights = halo_weight[0]
    halo_part = jnp.dot(weights, boundary, preferred_element_type=jnp.float32)
    degree_one = 1.0 + tile_degree + jnp.sum(weights, axis=1, dtype=jnp.float32)
    aggregated = ((numerator + halo_part) / degree_one[:, None]).astype(jnp.bfloat16)
    adjacency = tile_matrix(values, coords, live_slots, own_ids, all_blocks)
    degree_two = 1.0 + jnp.sum(adjacency, axis=1, dtype=jnp.float32)
    partial_sums = jnp.dot(features, first_self, preferred_element_type=jnp.float32) + jnp.dot(
        aggregated, first_neighbour, preferred_element_type=jnp.float32
    )
    preact_all = lax.psum(partial_sums.astype(jnp.bfloat16), "feat").astype(jnp.float32)
    hidden_all = jax.nn.silu(preact_all).astype(jnp.bfloat16)
    hidden_own = lax.dynamic_slice_in_dim(hidden_all, own_start, own_rows, 0)
    layer_sum = jnp.dot(adjacency, hidden_all, preferred_element_type=jnp.float32)
    neighbour_mean = (layer_sum / degree_two[:, None]).astype(jnp.bfloat16)
    embedding = (
        jnp.dot(hidden_own, second_self, preferred_element_type=jnp.float32)
        + jnp.dot(neighbour_mean, second_neighbour, preferred_element_type=jnp.float32)
    ).astype(jnp.bfloat16)
    cot_scale = 1.0 / math.sqrt(part_rows * lax.axis_size("node"))
    cotangent = (
        upstream.astype(jnp.float32) * seed_flags[:, None].astype(jnp.float32) * cot_scale
    ).astype(jnp.bfloat16)
    grad_two_self = lax.dot_general(
        hidden_own, cotangent, contract, preferred_element_type=jnp.float32
    )
    grad_two_neigh = lax.dot_general(
        neighbour_mean, cotangent, contract, preferred_element_type=jnp.float32
    )
    scaled_grad = (
        lax.dot_general(cotangent, second_neighbour, against, preferred_element_type=jnp.float32)
        / degree_two[:, None]
    ).astype(jnp.bfloat16)
    own_term = lax.dot_general(cotangent, second_self, against, preferred_element_type=jnp.float32)
    spread_back = lax.dot_general(
        adjacency, scaled_grad, contract, preferred_element_type=jnp.float32
    )
    own_part = lax.dynamic_slice_in_dim(spread_back, own_start, own_rows, 0) + own_term
    grad_partial = lax.dynamic_update_slice_in_dim(spread_back, own_part, own_start, 0)
    grad_all, grad_two_self, grad_two_neigh = (
        lax.psum(grad_partial.astype(jnp.bfloat16), "feat").astype(jnp.float32),
        lax.psum(grad_two_self.astype(jnp.bfloat16), "feat").astype(jnp.float32),
        lax.psum(grad_two_neigh.astype(jnp.bfloat16), "feat").astype(jnp.float32),
    )
    grad_preact = (grad_all * silu_slope(preact_all)).astype(jnp.bfloat16)
    grad_one_self = lax.dot_general(
        features, grad_preact, contract, preferred_element_type=jnp.float32
    )
    grad_one_neigh = lax.dot_general(
        aggregated, grad_preact, contract, preferred_element_type=jnp.float32
    )
    summed = lax.psum((grad_one_self, grad_one_neigh, grad_two_self, grad_two_neigh), "node")
    return (embedding, summed[0], summed[1], summed[2], summed[3])


FUSED_NODES = 8
HALO_ROWS = 16
MESH_ID = pl.DeviceIdType.MESH


def nn(a, b):
    return jnp.dot(a, b, preferred_element_type=jnp.float32)


def nt(a, b):
    return lax.dot_general(a, b, (((1,), (1,)), ((), ())), preferred_element_type=jnp.float32)


def step_kernel(
    groups, nodes,
    feats, tvals, coords, count, hidx, hweight, w1s, w1n, w2s, w2n, upstream, flags,
    emb_o, g1_o, g2_o,
    x_v, tiles, tiles_t, coords_v, flags_v, hidx_s, hw_t, hw_v, w1s_v, w1n_v, w2s_v, w2n_v, up_v, slot_v, slot_s,
    adj, adj_t, numer, deg, agg, x_t, agg_t, cot, cot_t, scaled, grad_h,
    hsend, hrecv, psend, precv, pre, hid, mean, gpre,
    s1, r1s, comb1, r1z, g1fin, s2, r2s, comb2, r2z, g2fin,
    ld_sem, halo_ss, halo_rs, cot_ss, cot_rs, rs_ss, rs_rs, ag_ss, ag_rs,
    sib_ss, sib_rs, z_ss, z_rs, zg_ss, zg_rs, fg_ss, fg_rs, fw_ss, fw_rs,
):
    f = lax.axis_index("feat")
    n = lax.axis_index("node")
    zs = nodes // 2
    z, c = n // 2, n % 2
    rows, width = x_v.shape
    slots = tiles.shape[0] - 1
    side = tiles.shape[1]
    blocks = rows // side
    own = up_v.shape[0]
    units = w1s_v.shape[1]
    outs = w2s_v.shape[1]
    cap = hidx.shape[1]

    def local(src, dst, i):
        copy = pltpu.make_async_copy(src, dst, ld_sem.at[i])
        copy.start()
        return copy

    def remote(src, dst, ss, rs, where):
        return pltpu.make_async_remote_copy(
            src_ref=src, dst_ref=dst, send_sem=ss, recv_sem=rs,
            device_id=where, device_id_type=MESH_ID,
        )

    def feat_at(d):
        return lax.rem(f + d, groups)

    def feat_id(d):
        return {"feat": feat_at(d)}

    def z_at(d):
        return lax.rem(z + d, zs)

    def z_id(d):
        return {"node": z_at(d) * 2 + c}

    feat_a = f + 1 - 2 * lax.rem(f, 2)
    feat_b = lax.rem(f + 2, groups)
    feat_c = lax.rem(feat_a + 2, groups)

    def half(ref, p, k):
        size = own // 2
        return ref.at[pl.ds(pl.multiple_of(p * own + k * size, size), size)]

    def gather_copy(ref, ss, rs, i, p, k, target):
        piece = half(ref, p, k)
        copy = remote(piece, piece, ss.at[i], rs.at[i], {"feat": target})
        copy.start()
        return copy

    def gather_start(ref, ss, rs):
        return [
            gather_copy(ref, ss, rs, i, f, k, target)
            for i, (k, target) in enumerate(
                ((0, feat_a), (1, feat_b), (1, feat_a), (0, feat_b))
            )
        ]

    def gather_forward(ref, ss, rs, copies):
        copies[0].wait_recv()
        copies.append(gather_copy(ref, ss, rs, 4, feat_a, 0, feat_b))
        copies[1].wait_recv()
        copies.append(gather_copy(ref, ss, rs, 5, feat_b, 1, feat_a))

    sib_id = {"node": z * 2 + (1 - c)}

    def own_rows(p):
        return pl.ds(pl.multiple_of(p * own, own), own)

    barrier = pltpu.get_barrier_semaphore()
    for d in range(1, groups):
        pl.semaphore_signal(barrier, inc=1, device_id=feat_id(d), device_id_type=MESH_ID)
    for d in range(1, nodes):
        pl.semaphore_signal(
            barrier, inc=1, device_id={"node": lax.rem(n + d, nodes)}, device_id_type=MESH_ID
        )

    ld_flags = local(flags, flags_v, 9)
    ld_up = local(upstream, up_v, 0)
    ld_hidx = local(hidx.at[0], hidx_s, 10)
    ld_coords = local(coords.at[0], coords_v, 11)
    ld_x = local(feats, x_v, 1)
    ld_t = local(tvals.at[0], tiles.at[pl.ds(0, slots)], 2)
    ld_hw = local(hweight.at[0], hw_t, 3)
    ld_1s = local(w1s, w1s_v, 4)
    ld_1n = local(w1n, w1n_v, 5)
    ld_2s = local(w2s, w2s_v, 6)
    ld_2n = local(w2n, w2n_v, 7)

    ld_coords.wait()
    key = coords_v[0:1, :] * blocks + coords_v[1:2, :]
    t_row = lax.broadcasted_iota(jnp.int32, (slots, slots), 0)
    t_col = lax.broadcasted_iota(jnp.int32, (slots, slots), 1)
    key = jnp.sum(jnp.where(t_row == t_col, key, 0), axis=1, keepdims=True)
    slot_id = lax.broadcasted_iota(jnp.int32, (slots, 128), 0)
    pair_id = lax.broadcasted_iota(jnp.int32, (slots, 128), 1)
    named = (key == pair_id) & (slot_id < count[0])
    slot_v[...] = jnp.broadcast_to(
        jnp.min(jnp.where(named, slot_id, slots), axis=0, keepdims=True), slot_v.shape
    )
    ld_slot = local(slot_v, slot_s, 8)
    tiles[slots] = jnp.zeros((side, side), jnp.bfloat16)
    tiles_t[slots] = jnp.zeros((side, side), jnp.bfloat16)

    scale = 1.0 / math.sqrt(rows * nodes)
    r_id = lax.broadcasted_iota(jnp.int32, (own, own), 0)
    c_id = lax.broadcasted_iota(jnp.int32, (own, own), 1)
    ld_flags.wait()
    picked = jnp.where((r_id == c_id) & (flags_v[...] != 0), 1.0, 0.0).astype(jnp.bfloat16)
    ld_up.wait()
    cot[own_rows(f), :] = (nn(picked, up_v[...]) * scale).astype(jnp.bfloat16)
    pl.semaphore_wait(barrier, groups - 1 + nodes - 1)
    cot_copies = gather_start(cot, cot_ss, cot_rs)

    row_id = lax.broadcasted_iota(jnp.int32, (HALO_ROWS, rows), 0)
    col_id = lax.broadcasted_iota(jnp.int32, (HALO_ROWS, rows), 1)
    parts = []
    ld_hidx.wait()
    for q in range(nodes):
        want = jnp.full((HALO_ROWS, rows), -1, jnp.int32)
        for k in range(cap):
            want = jnp.where(row_id == k, hidx_s[k, q], want)
        parts.append(jnp.where(want == col_id, 1.0, 0.0).astype(jnp.bfloat16))
    picks = jnp.concatenate(parts, axis=0)
    ld_x.wait()
    hsend[...] = nn(picks, x_v[...]).astype(jnp.bfloat16).reshape(hsend.shape)
    hrecv[n] = hsend[n]

    halo_copies = []
    for d in range(1, nodes):
        q = lax.rem(n + d, nodes)
        copy = remote(hsend.at[q], hrecv.at[n], halo_ss.at[d], halo_rs.at[d], {"node": q})
        copy.start()
        halo_copies.append(copy)
    ld_t.wait()
    ld_slot.wait()
    for r in range(blocks):
        for s in range(blocks):
            adj[r * side:(r + 1) * side, s * side:(s + 1) * side] = tiles[
                slot_s[0, r * blocks + s]
            ]
    ones_a = jnp.ones((rows, 128), jnp.bfloat16)

    @pl.loop(0, groups)
    def _(d):
        at = own_rows(d)
        tile_rows = adj[at, :]
        numer[at, :] = nn(tile_rows, x_v[...])
        deg[at, :] = 1.0 + nn(tile_rows, ones_a)

    gather_forward(cot, cot_ss, cot_rs, cot_copies)
    ld_hw.wait()
    hw_v[...] = hw_t[...].T
    ld_1s.wait()
    ld_1n.wait()
    for d, copy in enumerate(halo_copies):
        copy.wait_recv()
    halo = nodes * cap
    e_row = lax.broadcasted_iota(jnp.int32, (halo, nodes * HALO_ROWS), 0)
    e_col = lax.broadcasted_iota(jnp.int32, (halo, nodes * HALO_ROWS), 1)
    spread = (e_row // cap) * HALO_ROWS + e_row % cap
    unpad = jnp.where(spread == e_col, 1.0, 0.0).astype(jnp.bfloat16)
    bound = nn(unpad, hrecv[...].reshape(nodes * HALO_ROWS, width)).astype(jnp.bfloat16)
    ones_h = jnp.ones((halo, 128), jnp.bfloat16)

    def first_layer(p):
        at = own_rows(p)
        weights = hw_v[at, :]
        inverse = 1.0 / (deg[at, :] + nn(weights, ones_h))
        inverse = jnp.concatenate([inverse] * (width // 128), axis=1)
        mixed = ((numer[at, :] + nn(weights, bound)) * inverse).astype(jnp.bfloat16)
        agg[at, :] = mixed
        return nn(x_v[at, :], w1s_v[...]) + nn(mixed, w1n_v[...])

    rs_copies = []
    for d in range(1, groups):
        psend[d] = first_layer(feat_at(d)).astype(jnp.bfloat16)
        copy = remote(psend.at[d], precv.at[d], rs_ss.at[d], rs_rs.at[d], feat_id(d))
        copy.start()
        rs_copies.append(copy)
    total = first_layer(f)

    for copy in rs_copies:
        copy.wait_recv()
    for d in range(1, groups):
        total = total + precv[d].astype(jnp.float32)
    pre[own_rows(f), :] = total.astype(jnp.bfloat16)
    ag_copies = gather_start(pre, ag_ss, ag_rs)

    for k in range(groups):
        at = slice(k * own, (k + 1) * own)
        x_t[:, at] = x_v[at, :].T
    gather_forward(pre, ag_ss, ag_rs, ag_copies)
    for k in range(groups):
        at = slice(k * own, (k + 1) * own)
        agg_t[:, at] = agg[at, :].T

    for t in range(slots):
        tiles_t[t] = tiles[t].T
    for r in range(blocks):
        for s in range(blocks):
            adj_t[s * side:(s + 1) * side, r * side:(r + 1) * side] = tiles_t[
                slot_s[0, r * blocks + s]
            ]
    ld_2s.wait()
    ld_2n.wait()
    for copy in cot_copies[2:]:
        copy.wait_recv()
    for k in range(groups):
        at = slice(k * own, (k + 1) * own)
        cot_t[:, at] = cot[at, :].T

    @pl.loop(0, groups)
    def _(d):
        at = own_rows(d)
        inverse = 1.0 / deg[at, :]
        deg[at, :] = inverse
        inverse = jnp.concatenate([inverse] * (units // 128), axis=1)
        scaled[at, :] = (nt(cot[at, :], w2n_v[...]) * inverse).astype(jnp.bfloat16)

    @pl.loop(0, groups)
    def _(d):
        at = own_rows(d)
        grad_h[at, :] = nt(cot[at, :], w2s_v[...]) + nn(adj_t[at, :], scaled[...])

    def activate(p):
        at = own_rows(p)
        value = pre[at, :].astype(jnp.float32)
        sigm = jax.nn.sigmoid(value)
        hid[at, :] = (value * sigm).astype(jnp.bfloat16)
        slope = sigm * (1.0 + value * (1.0 - sigm))
        gpre[at, :] = (grad_h[at, :] * slope).astype(jnp.bfloat16)

    activate(f)
    for arrived, p in (((2,), feat_a), ((3,), feat_b), ((4, 5), feat_c)):
        for i in arrived:
            ag_copies[i].wait_recv()
        activate(p)

    piece = width // nodes
    for k, lhs in enumerate((x_t, agg_t)):
        grad = nn(lhs[...], gpre[...])
        for q in range(nodes):
            s1[q % 2, q // 2, k * piece:(k + 1) * piece, :] = grad[
                q * piece:(q + 1) * piece
            ].astype(jnp.bfloat16)
    sib1 = remote(s1.at[1 - c], r1s, sib_ss.at[0], sib_rs.at[0], sib_id)
    sib1.start()

    @pl.loop(0, groups)
    def _(d):
        at = own_rows(d)
        inverse = jnp.concatenate([deg[at, :]] * (units // 128), axis=1)
        mean[at, :] = (nn(adj[at, :], hid[...]) * inverse).astype(jnp.bfloat16)

    share = outs // groups
    bit = share // nodes
    cot_rows = cot_t[pl.ds(pl.multiple_of(f * share, share), share), :]
    both = (nn(cot_rows, hid[...]), nn(cot_rows, mean[...]))
    for q in range(nodes):
        s2[q % 2, q // 2] = jnp.concatenate(
            [grad[q * bit:(q + 1) * bit] for grad in both], axis=0
        ).astype(jnp.bfloat16)
    sib2 = remote(s2.at[1 - c], r2s, sib_ss.at[1], sib_rs.at[1], sib_id)
    sib2.start()

    z_copies = [None, None]
    for i, sib, mine, theirs, comb, dest in (
        (1, sib2, s2, r2s, comb2, r2z),
        (0, sib1, s1, r1s, comb1, r1z),
    ):
        sib.wait_recv()
        comb[...] = (mine[c].astype(jnp.float32) + theirs[...].astype(jnp.float32)).astype(
            jnp.bfloat16
        )
        batch = []
        for d in range(1, zs):
            copy = remote(
                comb.at[z_at(d)], dest.at[d], z_ss.at[i, d], z_rs.at[i, d], z_id(d)
            )
            copy.start()
            batch.append(copy)
        z_copies[i] = batch

    at = own_rows(f)
    emb_o[...] = (nn(hid[at, :], w2s_v[...]) + nn(mean[at, :], w2n_v[...])).astype(jnp.bfloat16)

    gathers = [None, None]
    for i, comb, dest, final in (
        (1, comb2, r2z, g2fin.at[f, c]),
        (0, comb1, r1z, g1fin.at[c]),
    ):
        total = comb[z].astype(jnp.float32)
        for d in range(1, zs):
            z_copies[i][d - 1].wait_recv()
            total = total + dest[d].astype(jnp.float32)
        if i == 0:
            g1fin[c, z] = total.astype(jnp.bfloat16)
        else:
            g2fin[f, c, z] = total.astype(jnp.bfloat16)
        batch = []
        for d in range(1, zs):
            copy = remote(
                final.at[z], final.at[z], zg_ss.at[i, d], zg_rs.at[i, d], z_id(d)
            )
            copy.start()
            batch.append(copy)
        gathers[i] = batch

    def forward(ref, i):
        copy = remote(ref, ref, fw_ss.at[i], fw_rs.at[i], sib_id)
        copy.start()
        return copy

    forwards = [forward(g1fin.at[c, z], 0)]
    for copy in gathers[1]:
        copy.wait_recv()
    feat_copies = []
    for d in range(1, groups):
        mine = g2fin.at[f, c]
        copy = remote(mine, mine, fg_ss.at[d], fg_rs.at[d], feat_id(d))
        copy.start()
        feat_copies.append(copy)
    forwards.append(forward(g2fin.at[f, c], 1))
    for d in range(1, zs):
        gathers[0][d - 1].wait_recv()
        forwards.append(forward(g1fin.at[c, z_at(zs - d)], 1 + d))
    for d in range(1, groups):
        feat_copies[d - 1].wait_recv()
        forwards.append(forward(g2fin.at[feat_at(groups - d), c], zs + d))
    for copy in forwards:
        copy.wait_recv()

    g1_o[...] = g1fin[...]
    g2_o[...] = g2fin[...]
    for copy in halo_copies + cot_copies + rs_copies + ag_copies + [sib1, sib2]:
        copy.wait_send()
    for batch in z_copies + gathers:
        for copy in batch:
            copy.wait_send()
    for copy in feat_copies + forwards:
        copy.wait_send()


def finish_kernel(
    groups, nodes, g1, g2, emb, emb_o, g1s_o, g1n_o, g2s_o, g2n_o, v1s, v1n, v2s, v2n, sems
):
    piece = g1.shape[2] // 2
    bit = g2.shape[3] // 2
    copies = []

    def out(src, dst):
        copy = pltpu.make_async_copy(src, dst, sems.at[len(copies)])
        copy.start()
        copies.append(copy)

    out(emb, emb_o)
    for k, (val, dst) in enumerate(((v1s, g1s_o), (v1n, g1n_o))):
        for q in range(nodes):
            val[q * piece:(q + 1) * piece, :] = g1[
                q % 2, q // 2, k * piece:(k + 1) * piece, :
            ].astype(jnp.float32)
        out(val, dst)
    for k, (val, dst) in enumerate(((v2s, g2s_o), (v2n, g2n_o))):
        val[...] = jnp.concatenate(
            [
                g2[g, q % 2, q // 2].astype(jnp.float32)[k * bit:(k + 1) * bit]
                for g in range(groups)
                for q in range(nodes)
            ],
            axis=0,
        ).T
        out(val, dst)
    for copy in copies:
        copy.wait()


def fused_step(
    groups, nodes, features, tile_values, tile_coords, tile_count, halo_index, halo_weight,
    first_self, first_neighbour, second_self, second_neighbour, upstream, seed_flags,
):
    rows, width = features.shape
    slots, side = tile_values.shape[1], tile_values.shape[2]
    halo = halo_weight.shape[2]
    own, outs = upstream.shape
    units = first_self.shape[1]
    zs = nodes // 2
    piece = 2 * width // nodes
    bit = 2 * outs // groups // nodes
    b16, f32 = jnp.bfloat16, jnp.float32
    vmem, hbm, smem = (
        pl.BlockSpec(memory_space=kind) for kind in (pltpu.VMEM, pltpu.HBM, pltpu.SMEM)
    )
    dma = pltpu.SemaphoreType.DMA
    scratch = [
        pltpu.VMEM((rows, width), b16),
        pltpu.VMEM((slots + 1, side, side), b16),
        pltpu.VMEM((slots + 1, side, side), b16),
        pltpu.VMEM((2, slots), jnp.int32),
        pltpu.VMEM((1, own), jnp.int32),
        pltpu.SMEM(halo_index.shape[:0:-1], jnp.int32),
        pltpu.VMEM((halo, rows), b16),
        pltpu.VMEM((rows, halo), b16),
        pltpu.VMEM((width, units), b16),
        pltpu.VMEM((width, units), b16),
        pltpu.VMEM((units, outs), b16),
        pltpu.VMEM((units, outs), b16),
        pltpu.VMEM((own, outs), b16),
        pltpu.VMEM((8, 128), jnp.int32),
        pltpu.SMEM((8, 128), jnp.int32),
        pltpu.VMEM((rows, rows), b16),
        pltpu.VMEM((rows, rows), b16),
        pltpu.VMEM((rows, width), f32),
        pltpu.VMEM((rows, 128), f32),
        pltpu.VMEM((rows, width), b16),
        pltpu.VMEM((width, rows), b16),
        pltpu.VMEM((width, rows), b16),
        pltpu.VMEM((rows, outs), b16),
        pltpu.VMEM((outs, rows), b16),
        pltpu.VMEM((rows, units), b16),
        pltpu.VMEM((rows, units), f32),
        pltpu.VMEM((nodes, HALO_ROWS, width), b16),
        pltpu.VMEM((nodes, HALO_ROWS, width), b16),
        pltpu.VMEM((groups, own, units), b16),
        pltpu.VMEM((groups, own, units), b16),
        pltpu.VMEM((rows, units), b16),
        pltpu.VMEM((rows, units), b16),
        pltpu.VMEM((rows, units), b16),
        pltpu.VMEM((rows, units), b16),
        pltpu.VMEM((2, zs, piece, units), b16),
        pltpu.VMEM((zs, piece, units), b16),
        pltpu.VMEM((zs, piece, units), b16),
        pltpu.VMEM((zs, piece, units), b16),
        pltpu.VMEM((2, zs, piece, units), b16),
        pltpu.VMEM((2, zs, bit, units), b16),
        pltpu.VMEM((zs, bit, units), b16),
        pltpu.VMEM((zs, bit, units), b16),
        pltpu.VMEM((zs, bit, units), b16),
        pltpu.VMEM((groups, 2, zs, bit, units), b16),
        dma((12,)),
        dma((nodes,)), dma((nodes,)),
        dma((6,)), dma((6,)),
        dma((groups,)), dma((groups,)),
        dma((6,)), dma((6,)),
        dma((2,)), dma((2,)),
        dma((2, zs)), dma((2, zs)),
        dma((2, zs)), dma((2, zs)),
        dma((groups,)), dma((groups,)),
        dma((zs + groups,)), dma((zs + groups,)),
    ]
    embedding, g1, g2 = pl.pallas_call(
        functools.partial(step_kernel, groups, nodes),
        out_shape=(
            jax.ShapeDtypeStruct((own, outs), b16),
            jax.ShapeDtypeStruct((2, zs, piece, units), b16),
            jax.ShapeDtypeStruct((groups, 2, zs, bit, units), b16),
        ),
        in_specs=[hbm, hbm, hbm, smem] + [hbm] * 8,
        out_specs=(vmem,) * 3,
        scratch_shapes=scratch,
        compiler_params=pltpu.CompilerParams(
            collective_id=0, has_side_effects=True, vmem_limit_bytes=56 * 1024 * 1024
        ),
    )(
        features, tile_values, jnp.swapaxes(tile_coords, 1, 2), tile_count,
        jnp.swapaxes(halo_index, 1, 2), jnp.swapaxes(halo_weight, 1, 2), first_self,
        first_neighbour, second_self, second_neighbour, upstream, seed_flags.reshape(1, own),
    )
    return pl.pallas_call(
        functools.partial(finish_kernel, groups, nodes),
        out_shape=(
            jax.ShapeDtypeStruct((own, outs), b16),
            jax.ShapeDtypeStruct((width, units), f32),
            jax.ShapeDtypeStruct((width, units), f32),
            jax.ShapeDtypeStruct((units, outs), f32),
            jax.ShapeDtypeStruct((units, outs), f32),
        ),
        in_specs=[vmem] * 3,
        out_specs=(hbm,) * 5,
        scratch_shapes=[
            pltpu.VMEM((width, units), f32),
            pltpu.VMEM((width, units), f32),
            pltpu.VMEM((units, outs), f32),
            pltpu.VMEM((units, outs), f32),
            dma((5,)),
        ],
    )(g1, g2, embedding)


def solution(mesh):
    groups, nodes = mesh.shape["feat"], mesh.shape["node"]
    step = functools.partial(fused_step, groups, nodes) if (groups, nodes) == (4, FUSED_NODES) else on_device
    in_specs = (
        P("node", "feat"),
        P("node", None, None, None),
        P("node", None, None),
        P("node"),
        P("node", None, None),
        P("node", None, None),
        P("feat", None),
        P("feat", None),
        P(),
        P(),
        P(("node", "feat"), None),
        P(("node", "feat")),
    )
    out_specs = (P(("node", "feat"), None), P("feat", None), P("feat", None), P(), P())
    return jax.shard_map(
        step, mesh=mesh, in_specs=in_specs, out_specs=out_specs, check_vma=False
    )
```
